32 devices in a mesh: ens: 2 (over x), bin: 16 (over z, y, core).
Axes of the slice: x: 2, y: 2, z: 4, core: 2. Of those that a mesh axis runs over, the one named last changes fastest.
Arguments:
- spectrum: bfloat16 [1536, 16, 512], P(('ens', 'bin')), parts along dimension 0, may hold values from 0.049804688 to 2
- land_mask: int32 [16, 512], replicated, may hold values 0 or 1
- depth_class: int32 [16, 512], replicated, may hold values from 0 to 7
- upwind_signs: int32 [2, 768], replicated, may hold values from -1 to 1, as said below
- group_speed: float32 [8, 24], replicated, may hold values from 0.2 to 0.7
- speed_ratio: float32 [8, 24], replicated, may hold values from 0.5 to 1
- mixing: bfloat16 [768, 768], replicated, may hold values from -0.0546875 to 0.0546875
- growth: float32 [768], replicated, may hold values from 0.01 to 0.08
- wind_speed: float32 [32, 512], P('ens'), parts along dimension 0, may hold values from 0.5 to 2
- water_depth: float32 [8], replicated, may hold values from 1 to 4
- currents: float32 [4, 16, 512], P('ens', 'bin'), parts along dimension 0, may hold values from -6 to 6
Outputs:
- spectrum_next: bfloat16 [1536, 16, 512], P(('ens', 'bin')), parts along dimension 0
- currents_next: float32 [4, 16, 512], P('ens', 'bin'), parts along dimension 0
The draws below stay inside these ranges and needn't reach their ends.
There are 2 independent parts, one for each index of `ens`. The reference program is written for one: setup_inputs(seed, part) draws one part's arguments, and reference() takes and returns one part's arrays. A program takes and returns all parts, laid end to end along the dimension named above; an argument that names none is the same for every part. Nothing has to cross between parts.
Inputs may be any that keep to these rules, and one draw needn't show every extreme that they name: `upwind_signs`: each entry is -1 or +1.
All inputs are finite; a program needn't handle non-finite values.
Results may differ from the reference program's by a relative error of at most 0.0052.
Values may be sent and summed in bfloat16 or wider, within the bound.
A program may use at most 64 MiB of HBM per device.

```python
import math
import jax
import jax.numpy as jnp
from jax import lax

NDIR = 32
NFREQ = 24
BINS = 768
NCLASS = 8
SUBS = 8
NY = 512
NX = 16


def draw_upwind_signs(key, part):
    key = jax.random.fold_in(key, 5)
    coins = jax.random.randint(key, (2, BINS), 0, 2)
    return (2 * coins - 1).astype(jnp.int32)


def set_ends(result, own_key, smallest, largest):
    extent = result.shape
    index_at = [jax.random.randint(jax.random.fold_in(own_key, axis), (), 0, extent[axis]) for axis in range(len(extent))]
    result = result.at[tuple(index_at)].set(smallest)
    longest = extent.index(max(extent))
    index_at[longest] = (index_at[longest] + 1) % extent[longest]
    return result.at[tuple(index_at)].set(largest)


def steps_of(rng, dims, pieces, least, top_value):
    level, own = 1.0, jax.random.fold_in(rng, 6)
    for dim, shards_of in pieces:
        steps = jnp.exp(jax.random.uniform(jax.random.fold_in(own, dim), (shards_of,), jnp.float32, least / len(pieces), top_value / len(pieces)))
        level = level * jnp.repeat(steps, dims[dim] // shards_of).reshape([-1 if axis == dim else 1 for axis in range(len(dims))])
    return level


def centred(rng, extent, scale, limit, shards=(), kind=jnp.bfloat16):
    level = steps_of(rng, extent, shards, -0.22, 0.18) if shards else 1.0
    result = jax.random.normal(rng, extent, jnp.float32) * scale * level
    return jnp.minimum(jnp.maximum(result, -limit), limit).astype(kind)


def setup_inputs(seed: int = 0, part: int = 0) -> dict:
    splits = jax.random.split(jax.random.key(seed), 12)
    own_keys = jax.random.split(jax.random.fold_in(splits[11], part), 12)
    spectrum = jnp.clip(jnp.exp(math.log(2.0) - 3.6927934 * jax.random.uniform(own_keys[0], (BINS, NX, NY), jnp.float32) ** steps_of(own_keys[0], (BINS, NX, NY), ((0, 16),), -0.2, 0.2)), 0.049804688, 2.0).astype(jnp.bfloat16)
    land_mask = set_ends((jax.random.randint(splits[1], (NX, NY), 0, 8) < 7).astype(jnp.int32), jax.random.fold_in(splits[1], 1), 0, 1)
    depth_class = set_ends(jax.random.randint(splits[2], (NX, NY), 0, NCLASS), jax.random.fold_in(splits[2], 1), 0, NCLASS - 1).astype(jnp.int32)
    upwind_signs = draw_upwind_signs(jax.random.fold_in(splits[11], 71), part)
    group_speed = jnp.clip(jnp.exp(jax.random.uniform(splits[4], (NCLASS, NFREQ), jnp.float32, math.log(0.2), math.log(0.7))), 0.2, 0.7)
    speed_ratio = jnp.clip(jax.random.uniform(splits[5], (NCLASS, NFREQ), jnp.float32, 0.5, 1.0), 0.5, 1.0)
    mixing = centred(splits[6], (BINS, BINS), (16 * BINS) ** -0.5, 0.0546875)
    growth = jnp.clip(jnp.exp(jax.random.uniform(splits[7], (BINS,), jnp.float32, math.log(0.01), math.log(0.08))), 0.01, 0.08)
    wind_speed = jnp.clip(jax.random.uniform(own_keys[8], (NX, NY), jnp.float32, 0.5, 2.0), 0.5, 2.0)
    water_depth = jnp.clip(jnp.exp(jax.random.uniform(splits[9], (NCLASS,), jnp.float32, math.log(1.0), math.log(4.0))), 1.0, 4.0)
    currents = centred(own_keys[10], (2, NX, NY), 1.0, 6.0, ((1, 16),), jnp.float32)
    return {"spectrum": spectrum, "land_mask": land_mask, "depth_class": depth_class, "upwind_signs": upwind_signs, "group_speed": group_speed, "speed_ratio": speed_ratio, "mixing": mixing, "growth": growth, "wind_speed": wind_speed, "water_depth": water_depth, "currents": currents}


STRESS_SCALE = 0.0625


def angle_of(direction):
    return (2.0 * math.pi) * (direction + 0.5) / NDIR


def from_lower(field, axis):
    width = [(0, 0)] * field.ndim
    width[axis] = (1, 0)
    padded = jnp.pad(field, width)
    return lax.slice_in_dim(padded, 0, field.shape[axis], axis=axis)


def from_upper(field, axis):
    width = [(0, 0)] * field.ndim
    width[axis] = (0, 1)
    padded = jnp.pad(field, width)
    return lax.slice_in_dim(padded, 1, field.shape[axis] + 1, axis=axis)


def upwind_step(energy, celerity, cos_abs, sin_abs, sign_x, sign_y, maskf):
    axis_x = energy.ndim - 2
    axis_y = energy.ndim - 1
    flux_x = maskf * ((sign_x * celerity * cos_abs) * energy)
    flux_y = maskf * ((sign_y * celerity * sin_abs) * energy)
    diff_x = jnp.where(sign_x > 0, flux_x - from_lower(flux_x, axis_x), from_upper(flux_x, axis_x) - flux_x)
    diff_y = jnp.where(sign_y > 0, flux_y - from_lower(flux_y, axis_y), from_upper(flux_y, axis_y) - flux_y)
    return maskf * ((energy - diff_x) - diff_y)


def integrate(energy, mixing, growth, wind_flat):
    for substep in range(SUBS):
        rounded = energy.astype(jnp.bfloat16)
        energy = energy + jnp.dot(mixing, rounded, preferred_element_type=jnp.float32) + growth[:, None] * wind_flat[None, :] * energy
    return energy.astype(jnp.bfloat16)


def radiation(fresh, ratio_map):
    energy = fresh.astype(jnp.float32).reshape(NDIR, NFREQ, -1)
    theta = angle_of(jnp.arange(NDIR, dtype=jnp.float32))
    cosine = jnp.cos(theta)
    sine = jnp.sin(theta)
    coeff = jnp.stack([cosine * cosine + 1.0, cosine * sine, sine * sine + 1.0])
    weighted = jnp.einsum('cd,dfn->cfn', coeff, energy, precision=lax.Precision.HIGHEST)
    total = jnp.sum(energy, axis=(0, 1))
    flat_ratio = ratio_map.reshape(NFREQ, -1)
    offset = jnp.array([0.5, 0.0, 0.5], dtype=jnp.float32)
    stress = (jnp.sum(flat_ratio[None] * weighted, axis=1) - offset[:, None] * total[None]) * STRESS_SCALE
    return stress.reshape(3, fresh.shape[1], fresh.shape[2])


def forcing(stress_wide, currents, depth_map, maskf):
    slope_x = (stress_wide[:, 2:] - stress_wide[:, :-2]) * 0.5
    inner = stress_wide[:, 1:-1]
    padded_y = jnp.pad(inner, ((0, 0), (0, 0), (1, 1)))
    slope_y = (padded_y[:, :, 2:] - padded_y[:, :, :-2]) * 0.5
    force = jnp.stack([-(slope_x[0] + slope_y[1]), -(slope_x[1] + slope_y[2])])
    return maskf * (currents + force / depth_map)


def reference(spectrum, land_mask, depth_class, upwind_signs, group_speed, speed_ratio, mixing, growth, wind_speed, water_depth, currents):
    maskf = land_mask.astype(jnp.float32)
    bin_ids = jnp.arange(BINS, dtype=jnp.int32)
    theta = angle_of((bin_ids // NFREQ).astype(jnp.float32))
    freq_ids = bin_ids % NFREQ
    speed_cells = jnp.moveaxis(jnp.take(group_speed, depth_class, axis=0), 2, 0)
    signs_float = upwind_signs.astype(jnp.float32)

    def one_bin(item):
        energy, freq, cos_abs, sin_abs, sign_x, sign_y = item
        celerity = jnp.take(speed_cells, freq, axis=0)
        return upwind_step(energy.astype(jnp.float32), celerity, cos_abs, sin_abs, sign_x, sign_y, maskf)

    moved = lax.map(one_bin, (spectrum, freq_ids, jnp.abs(jnp.cos(theta)), jnp.abs(jnp.sin(theta)), signs_float[0], signs_float[1])).astype(jnp.bfloat16)
    fresh = integrate(moved.astype(jnp.float32).reshape(BINS, -1), mixing, growth, wind_speed.reshape(-1)).reshape(BINS, NX, NY)
    ratio_map = jnp.moveaxis(jnp.take(speed_ratio, depth_class, axis=0), 2, 0)
    stress = radiation(fresh, ratio_map)
    stress_wide = jnp.pad(stress, ((0, 0), (1, 1), (0, 0)))
    depth_map = jnp.take(water_depth, depth_class, axis=0)
    return fresh, forcing(stress_wide, currents, depth_map, maskf)
```

```python
import functools
import math

import jax
import jax.numpy as jnp
import numpy as np
from jax import lax
from jax.experimental import pallas as pl
from jax.experimental.pallas import tpu as pltpu
from jax.sharding import PartitionSpec as P

NDIR = 32
NFREQ = 24
NCLASS = 8
SUBS = 8


STRESS_SCALE = 0.0625


def extended(shard, sides, width):
    for axis, dim in sides:
        peers, length = (lax.axis_size(axis), shard.shape[dim])
        up = [(i, (i + 1) % peers) for i in range(peers - 1)]
        down = [(j, i) for i, j in up]
        last = lax.slice_in_dim(shard, length - width, length, axis=dim)
        initial = lax.slice_in_dim(shard, 0, width, axis=dim)
        before = lax.ppermute(last, axis, up)
        after = lax.ppermute(initial, axis, down)
        shard = jnp.concatenate([before, shard, after], axis=dim)
    return shard


def angle_of(direction):
    return 2.0 * math.pi * (direction + 0.5) / NDIR


def from_lower(field, axis):
    width = [(0, 0)] * field.ndim
    width[axis] = (1, 0)
    padded = jnp.pad(field, width)
    return lax.slice_in_dim(padded, 0, field.shape[axis], axis=axis)


def from_upper(field, axis):
    width = [(0, 0)] * field.ndim
    width[axis] = (0, 1)
    padded = jnp.pad(field, width)
    return lax.slice_in_dim(padded, 1, field.shape[axis] + 1, axis=axis)


def upwind_step(energy, celerity, cos_abs, sin_abs, sign_x, sign_y, maskf):
    axis_x = energy.ndim - 2
    axis_y = energy.ndim - 1
    flux_x = maskf * (sign_x * celerity * cos_abs * energy)
    flux_y = maskf * (sign_y * celerity * sin_abs * energy)
    diff_x = jnp.where(
        sign_x > 0, flux_x - from_lower(flux_x, axis_x), from_upper(flux_x, axis_x) - flux_x
    )
    diff_y = jnp.where(
        sign_y > 0, flux_y - from_lower(flux_y, axis_y), from_upper(flux_y, axis_y) - flux_y
    )
    return maskf * (energy - diff_x - diff_y)


def integrate(energy, mixing, growth, wind_flat):
    for substep in range(SUBS):
        rounded = energy.astype(jnp.bfloat16)
        energy = (
            energy
            + jnp.dot(mixing, rounded, preferred_element_type=jnp.float32)
            + growth[:, None] * wind_flat[None, :] * energy
        )
    return energy.astype(jnp.bfloat16)


def radiation(fresh, ratio_map):
    energy = fresh.astype(jnp.float32).reshape(NDIR, NFREQ, -1)
    theta = angle_of(jnp.arange(NDIR, dtype=jnp.float32))
    cosine = jnp.cos(theta)
    sine = jnp.sin(theta)
    coeff = jnp.stack([cosine * cosine + 1.0, cosine * sine, sine * sine + 1.0])
    weighted = jnp.einsum("cd,dfn->cfn", coeff, energy, precision=lax.Precision.HIGHEST)
    total = jnp.sum(energy, axis=(0, 1))
    flat_ratio = ratio_map.reshape(NFREQ, -1)
    offset = jnp.array([0.5, 0.0, 0.5], dtype=jnp.float32)
    stress = (
        jnp.sum(flat_ratio[None] * weighted, axis=1) - offset[:, None] * total[None]
    ) * STRESS_SCALE
    return stress.reshape(3, fresh.shape[1], fresh.shape[2])


def forcing(stress_wide, currents, depth_map, maskf):
    slope_x = (stress_wide[:, 2:] - stress_wide[:, :-2]) * 0.5
    inner = stress_wide[:, 1:-1]
    padded_y = jnp.pad(inner, ((0, 0), (0, 0), (1, 1)))
    slope_y = (padded_y[:, :, 2:] - padded_y[:, :, :-2]) * 0.5
    force = jnp.stack([-(slope_x[0] + slope_y[1]), -(slope_x[1] + slope_y[2])])
    return maskf * (currents + force / depth_map)


def local(
    spectrum,
    land_mask,
    depth_class,
    upwind_signs,
    group_speed,
    speed_ratio,
    mixing,
    growth,
    wind_speed,
    water_depth,
    currents,
):
    bin_local = spectrum.shape[0]
    own_rows = currents.shape[1]
    device_index = lax.axis_index("bin")
    bin_ids = device_index * bin_local + jnp.arange(bin_local, dtype=jnp.int32)
    theta = angle_of((bin_ids // NFREQ).astype(jnp.float32))
    cos_abs = jnp.abs(jnp.cos(theta))[:, None, None]
    sin_abs = jnp.abs(jnp.sin(theta))[:, None, None]
    freq_select = (
        (bin_ids % NFREQ)[:, None] == jnp.arange(NFREQ, dtype=jnp.int32)[None, :]
    ).astype(jnp.float32)
    speed_table = jnp.dot(group_speed, freq_select.T, precision=lax.Precision.HIGHEST)
    classes = (depth_class[None] == jnp.arange(NCLASS, dtype=jnp.int32)[:, None, None]).astype(
        jnp.float32
    )
    celerity = jnp.einsum("kb,kxy->bxy", speed_table, classes, precision=lax.Precision.HIGHEST)
    upwind = lax.dynamic_slice_in_dim(upwind_signs, device_index * bin_local, bin_local, 1).astype(
        jnp.float32
    )
    maskf = land_mask.astype(jnp.float32)
    moved = upwind_step(
        spectrum.astype(jnp.float32),
        celerity,
        cos_abs,
        sin_abs,
        upwind[0][:, None, None],
        upwind[1][:, None, None],
        maskf,
    ).astype(jnp.bfloat16)
    first_row = device_index * own_rows
    wind_rows = lax.dynamic_slice_in_dim(wind_speed, first_row, own_rows, 0)
    class_rows = lax.dynamic_slice_in_dim(depth_class, first_row, own_rows, 0)
    mask_own = lax.dynamic_slice_in_dim(maskf, first_row, own_rows, 0)
    ratio_classes = (class_rows[None] == jnp.arange(NCLASS, dtype=jnp.int32)[:, None, None]).astype(
        jnp.float32
    )
    ratio_map = jnp.einsum(
        "kf,kxy->fxy", speed_ratio, ratio_classes, precision=lax.Precision.HIGHEST
    )

    def owner_step(received, wind_block):
        energy = received.astype(jnp.float32).reshape(received.shape[0], -1)
        return integrate(energy, mixing, growth, wind_block.reshape(-1)).reshape(received.shape)

    pieces = [(lax.all_to_all(moved, "bin", split_axis=1, concat_axis=0, tiled=True), wind_rows)]
    fresh = jnp.concatenate([owner_step(piece, wind_part) for piece, wind_part in pieces], axis=2)
    stress = extended(radiation(fresh, ratio_map), (("bin", 1),), 1)
    spectrum_next = lax.all_to_all(fresh, "bin", split_axis=0, concat_axis=1, tiled=True)
    depth_map = jnp.einsum("k,kxy->xy", water_depth, ratio_classes, precision=lax.Precision.HIGHEST)
    return (spectrum_next, forcing(stress, currents, depth_map, mask_own))


CHUNKS = 2
GROUP = 16
LANES = 128
COEF_ROWS = 160
MESH = pl.DeviceIdType.MESH
HIGHEST = lax.Precision.HIGHEST


def flipped(index, k, n):
    result, bit = 0, 1
    while bit < n:
        result = result + ((index // bit + k // bit) % 2) * bit
        bit *= 2
    return result


def stress_matrix():
    theta = angle_of(np.arange(NDIR, dtype=np.float64))
    cosine, sine = np.cos(theta), np.sin(theta)
    weights = np.stack([cosine * cosine + 1.0, cosine * sine, sine * sine + 1.0])
    full = np.einsum("cd,fg->cfdg", weights, np.eye(NFREQ)).reshape(3 * NFREQ, NDIR * NFREQ)
    high = full.astype(jnp.bfloat16)
    low = (full - high.astype(np.float64)).astype(jnp.bfloat16)
    table = np.zeros((COEF_ROWS, NDIR * NFREQ), dtype=jnp.bfloat16)
    table[: 3 * NFREQ] = high
    table[3 * NFREQ : 6 * NFREQ] = low
    table[6 * NFREQ] = 1.0
    return table


def trig_table():
    theta = angle_of(np.arange(NDIR, dtype=np.float64))
    return np.abs(np.stack([np.cos(theta), np.sin(theta)])).astype(np.float32)


def wide(tile, width):
    return jnp.concatenate([tile] * (width // LANES), axis=1)


def fused_kernel(
    n,
    spectrum_hbm,
    mask_ref,
    class_ref,
    signs_ref,
    speed_ref,
    ratio_ref,
    mixing_hbm,
    growth_ref,
    wind_ref,
    depth_ref,
    currents_ref,
    trig_ref,
    coef_hbm,
    out_ref,
    currents_out,
    spectrum_v,
    mixing_v,
    coef_v,
    perm,
    energy_v,
    flux,
    speed_cols,
    sign_cols,
    growth_cols,
    ratio_map,
    send,
    state,
    total,
    back,
    stress,
    halo,
    load_sems,
    fwd_send,
    fwd_recv,
    ret_send,
    ret_recv,
    halo_send,
    halo_recv,
):
    me = lax.axis_index("bin")
    nb, nx, ny = spectrum_v.shape
    bins = mixing_v.shape[0]
    width = ny // CHUNKS
    groups = nb // GROUP

    loads = [
        pltpu.make_async_copy(src, dst, load_sems.at[i])
        for i, (src, dst) in enumerate(
            [(spectrum_hbm, spectrum_v), (mixing_hbm, mixing_v), (coef_hbm, coef_v)]
        )
    ]
    for load in loads:
        load.start()
    barrier = pltpu.get_barrier_semaphore()

    def greet(k, carry):
        pl.semaphore_signal(
            barrier, inc=1, device_id={"bin": flipped(me, k, n)}, device_id_type=MESH
        )
        return carry

    lax.fori_loop(1, n, greet, 0)

    side = GROUP * nx
    row_id = lax.broadcasted_iota(jnp.int32, (side, side), 0)
    col_id = lax.broadcasted_iota(jnp.int32, (side, side), 1)
    perm[...] = jnp.where(
        (row_id // GROUP == col_id % nx) & (row_id % GROUP == col_id // nx), 1.0, 0.0
    ).astype(jnp.bfloat16)
    spread = jnp.where(
        lax.broadcasted_iota(jnp.int32, (NCLASS, NCLASS * LANES), 0)
        == lax.broadcasted_iota(jnp.int32, (NCLASS, NCLASS * LANES), 1) // LANES,
        1.0,
        0.0,
    )
    columns = lax.dot_general(
        speed_ref[...], spread, (((0,), (0,)), ((), ())), precision=HIGHEST,
        preferred_element_type=jnp.float32,
    )
    columns = jnp.concatenate([columns] * (nb // NFREQ), axis=0)
    for k in range(NCLASS):
        speed_cols[k] = columns[:, k * LANES : (k + 1) * LANES]
    pick = jnp.where(
        lax.broadcasted_iota(jnp.int32, (nb, bins), 1)
        == lax.broadcasted_iota(jnp.int32, (nb, bins), 0) + me * nb,
        1.0,
        0.0,
    ).astype(jnp.bfloat16)
    for axis in range(2):
        signs = jnp.broadcast_to(
            signs_ref[axis : axis + 1, :].astype(jnp.float32), (LANES, bins)
        ).astype(jnp.bfloat16)
        sign_cols[axis] = lax.dot_general(
            pick, signs, (((1,), (1,)), ((), ())), preferred_element_type=jnp.float32
        )
    per_dev = nb // NFREQ
    bin_row = lax.broadcasted_iota(jnp.int32, (nb, LANES), 0)
    for axis in range(2):
        column = jnp.zeros((nb, LANES), jnp.float32)
        for d in range(per_dev):
            column = jnp.where(bin_row // NFREQ == d, trig_ref[axis, me * per_dev + d], column)
        sign_cols[2 + axis] = column

    flux[0] = jnp.zeros((nb, ny), jnp.float32)
    flux[nx + 1] = jnp.zeros((nb, ny), jnp.float32)

    loads[0].wait()
    for g in range(groups):
        block = spectrum_v[g * GROUP : (g + 1) * GROUP].reshape(side, ny)
        turned = jnp.dot(perm[...], block, preferred_element_type=jnp.float32)
        energy_v[:, g * GROUP : (g + 1) * GROUP, :] = turned.astype(jnp.bfloat16).reshape(
            nx, GROUP, ny
        )

    def flux_row(i, carry):
        sea = jnp.where(mask_ref[pl.ds(i, 1), :] > 0, class_ref[pl.ds(i, 1), :], -1)
        sea = jnp.broadcast_to(sea, (GROUP, ny))
        for g in range(groups):
            rows = slice(g * GROUP, (g + 1) * GROUP)
            celerity = jnp.zeros((GROUP, ny), jnp.float32)
            for k in range(NCLASS):
                celerity = jnp.where(sea == k, wide(speed_cols[k, rows, :], ny), celerity)
            flux[i + 1, rows, :] = celerity * energy_v[i, rows, :].astype(jnp.float32)
        return carry

    lax.fori_loop(0, nx, flux_row, 0)
    pl.semaphore_wait(barrier, n - 1)

    def forward(c, k):
        return pltpu.make_async_remote_copy(
            src_ref=send.at[c, flipped(me, k, n)],
            dst_ref=state.at[c, 0, pl.ds(pl.multiple_of(me * nb, nb), nb), :],
            send_sem=fwd_send.at[c, k],
            recv_sem=fwd_recv.at[c, k],
            device_id={"bin": flipped(me, k, n)},
            device_id_type=MESH,
        )

    def backward(c, k):
        return pltpu.make_async_remote_copy(
            src_ref=state.at[c, 0, pl.ds(pl.multiple_of(flipped(me, k, n) * nb, nb), nb), :],
            dst_ref=back.at[c, me],
            send_sem=ret_send.at[c, k],
            recv_sem=ret_recv.at[c, k],
            device_id={"bin": flipped(me, k, n)},
            device_id_type=MESH,
        )

    lane = lax.broadcasted_iota(jnp.int32, (GROUP, ny), 1)

    def moved_row(t, carry):
        k = n - 1 - t
        j = flipped(me, k, n)
        maskf = mask_ref[pl.ds(j, 1), :].astype(jnp.float32)
        for g in range(groups):
            rows = slice(g * GROUP, (g + 1) * GROUP)
            sign_x = wide(sign_cols[0, rows, :], ny)
            sign_y = wide(sign_cols[1, rows, :], ny)
            cos_abs = wide(sign_cols[2, rows, :], ny)
            sin_abs = wide(sign_cols[3, rows, :], ny)
            here = flux[j + 1, rows, :]
            lower_y = jnp.where(lane == 0, 0.0, pltpu.roll(here, 1, 1))
            upper_y = jnp.where(lane == ny - 1, 0.0, pltpu.roll(here, ny - 1, 1))
            beside_x = jnp.where(sign_x > 0, flux[j, rows, :], flux[j + 2, rows, :])
            beside_y = jnp.where(sign_y > 0, lower_y, upper_y)
            energy = energy_v[j, rows, :].astype(jnp.float32)
            moved = maskf * (
                energy - cos_abs * (here - beside_x) - sin_abs * (here - beside_y)
            )
            moved = moved.astype(jnp.bfloat16)
            for c in range(CHUNKS):
                send[c, j, rows, :] = moved[:, c * width : (c + 1) * width]

        @pl.when(k > 0)
        def _():
            forward(0, k).start()

        return carry

    lax.fori_loop(0, n, moved_row, 0)
    for c in range(1, CHUNKS):

        def start_forward(t, carry):
            forward(c, n - 1 - t).start()
            return carry

        lax.fori_loop(0, n - 1, start_forward, 0)
    own = pl.ds(pl.multiple_of(me * nb, nb), nb)
    for c in range(CHUNKS):
        state[c, 0, own, :] = send[c, me]

    growth_cols[...] = jnp.broadcast_to(growth_ref[...], (LANES, bins)).T
    class_row = class_ref[pl.ds(me, 1), :]
    one_hot = jnp.where(
        lax.broadcasted_iota(jnp.int32, (NCLASS, ny), 0)
        == jnp.broadcast_to(class_row, (NCLASS, ny)),
        1.0,
        0.0,
    )
    ratio_map[...] = lax.dot_general(
        ratio_ref[...], one_hot, (((0,), (0,)), ((), ())), precision=HIGHEST,
        preferred_element_type=jnp.float32,
    )
    stress[...] = jnp.zeros_like(stress)

    @pl.when(me == 0)
    def _():
        halo[0] = jnp.zeros_like(halo[0])

    @pl.when(me == n - 1)
    def _():
        halo[1] = jnp.zeros_like(halo[1])

    loads[1].wait()
    loads[2].wait()

    tall = 256
    for c in range(CHUNKS):
        lanes = slice(c * width, (c + 1) * width)

        def wait_forward(k, carry):
            forward(c, k).wait_recv()
            return carry

        lax.fori_loop(1, n, wait_forward, 0)
        wind = wind_ref[pl.ds(me, 1), lanes]
        total[...] = state[c, 0].astype(jnp.float32)

        def substep(s, carry):
            now = s % 2
            rounded = state[c, now]
            for r in range(0, bins, tall):
                mixed = jnp.dot(
                    mixing_v[r : r + tall, :], rounded, preferred_element_type=jnp.float32
                )
                held = total[r : r + tall, :]
                held = held + mixed + wide(growth_cols[r : r + tall, :], width) * wind * held
                total[r : r + tall, :] = held
                state[c, 1 - now, r : r + tall, :] = held.astype(jnp.bfloat16)
            return carry

        lax.fori_loop(0, SUBS, substep, 0)

        def start_backward(t, carry):
            backward(c, n - 1 - t).start()
            return carry

        lax.fori_loop(0, n - 1, start_backward, 0)
        back[c, me] = state[c, 0, own, :]
        weighted = jnp.dot(coef_v[...], state[c, 0], preferred_element_type=jnp.float32)
        whole_sum = weighted[6 * NFREQ : 6 * NFREQ + 1, :]
        for comp, offset in enumerate((0.5, 0.0, 0.5)):
            first = comp * NFREQ
            second = (3 + comp) * NFREQ
            part = weighted[first : first + NFREQ, :] + weighted[second : second + NFREQ, :]
            part = jnp.sum(ratio_map[:, lanes] * part, axis=0, keepdims=True)
            stress[comp : comp + 1, lanes] = (part - offset * whole_sum) * STRESS_SCALE

    def to_next():
        return pltpu.make_async_remote_copy(
            src_ref=stress,
            dst_ref=halo.at[0],
            send_sem=halo_send.at[0],
            recv_sem=halo_recv.at[0],
            device_id={"bin": (me + 1) % n},
            device_id_type=MESH,
        )

    def to_previous():
        return pltpu.make_async_remote_copy(
            src_ref=stress,
            dst_ref=halo.at[1],
            send_sem=halo_send.at[1],
            recv_sem=halo_recv.at[1],
            device_id={"bin": (me + n - 1) % n},
            device_id_type=MESH,
        )

    @pl.when(me < n - 1)
    def _():
        to_next().start()

    @pl.when(me > 0)
    def _():
        to_previous().start()

    def turn_back(c):
        def wait_backward(k, carry):
            backward(c, k).wait_recv()
            return carry

        lax.fori_loop(1, n, wait_backward, 0)
        for g in range(groups):
            block = back[c, :, g * GROUP : (g + 1) * GROUP, :].reshape(side, width)
            turned = lax.dot_general(
                perm[...], block, (((0,), (0,)), ((), ())), preferred_element_type=jnp.float32
            )
            out_ref[g * GROUP : (g + 1) * GROUP, :, c * width : (c + 1) * width] = turned.astype(
                jnp.bfloat16
            ).reshape(GROUP, nx, width)

    for c in range(CHUNKS - 1):
        turn_back(c)

    @pl.when(me > 0)
    def _():
        to_next().wait_recv()

    @pl.when(me < n - 1)
    def _():
        to_previous().wait_recv()

    slope_x = (halo[1] - halo[0]) * 0.5
    mine = stress[...]
    lane8 = lax.broadcasted_iota(jnp.int32, mine.shape, 1)
    above = jnp.where(lane8 == ny - 1, 0.0, pltpu.roll(mine, ny - 1, 1))
    below = jnp.where(lane8 == 0, 0.0, pltpu.roll(mine, 1, 1))
    slope_y = (above - below) * 0.5
    depth = jnp.zeros((1, ny), jnp.float32)
    for k in range(NCLASS):
        depth = jnp.where(class_row == k, depth_ref[k], depth)
    sea_row = mask_ref[pl.ds(me, 1), :].astype(jnp.float32)
    for comp in range(2):
        force = -(slope_x[comp : comp + 1, :] + slope_y[comp + 1 : comp + 2, :])
        currents_out[comp] = sea_row * (currents_ref[comp] + force / depth)

    turn_back(CHUNKS - 1)

    def finish(k, carry):
        for c in range(CHUNKS):
            forward(c, k).wait_send()
            backward(c, k).wait_send()
        return carry

    lax.fori_loop(1, n, finish, 0)

    @pl.when(me < n - 1)
    def _():
        to_next().wait_send()

    @pl.when(me > 0)
    def _():
        to_previous().wait_send()


def fused(
    n,
    spectrum,
    land_mask,
    depth_class,
    upwind_signs,
    group_speed,
    speed_ratio,
    mixing,
    growth,
    wind_speed,
    water_depth,
    currents,
):
    nb, nx, ny = spectrum.shape
    bins = mixing.shape[0]
    width = ny // CHUNKS
    vmem = pl.BlockSpec(memory_space=pltpu.VMEM)
    smem = pl.BlockSpec(memory_space=pltpu.SMEM)
    anywhere = pl.BlockSpec(memory_space=pl.ANY)
    f32, bf16 = jnp.float32, jnp.bfloat16
    dma = pltpu.SemaphoreType.DMA
    return pl.pallas_call(
        functools.partial(fused_kernel, n),
        out_shape=(
            jax.ShapeDtypeStruct(spectrum.shape, bf16),
            jax.ShapeDtypeStruct(currents.shape, f32),
        ),
        in_specs=[
            anywhere, vmem, vmem, vmem, vmem, vmem, anywhere, vmem, vmem, smem, vmem, smem, anywhere,
        ],
        out_specs=(vmem, vmem),
        scratch_shapes=[
            pltpu.VMEM((nb, nx, ny), bf16),
            pltpu.VMEM((bins, bins), bf16),
            pltpu.VMEM((COEF_ROWS, bins), bf16),
            pltpu.VMEM((GROUP * nx, GROUP * nx), bf16),
            pltpu.VMEM((nx, nb, ny), bf16),
            pltpu.VMEM((nx + 2, nb, ny), f32),
            pltpu.VMEM((NCLASS, nb, LANES), f32),
            pltpu.VMEM((4, nb, LANES), f32),
            pltpu.VMEM((bins, LANES), f32),
            pltpu.VMEM((NFREQ, ny), f32),
            pltpu.VMEM((CHUNKS, nx, nb, width), bf16),
            pltpu.VMEM((CHUNKS, 2, bins, width), bf16),
            pltpu.VMEM((bins, width), f32),
            pltpu.VMEM((CHUNKS, nx, nb, width), bf16),
            pltpu.VMEM((8, ny), f32),
            pltpu.VMEM((2, 8, ny), f32),
            dma((3,)),
            dma((CHUNKS, n)),
            dma((CHUNKS, n)),
            dma((CHUNKS, n)),
            dma((CHUNKS, n)),
            dma((2,)),
            dma((2,)),
        ],
        compiler_params=pltpu.CompilerParams(
            collective_id=0, has_side_effects=True, vmem_limit_bytes=40 * 1024 * 1024
        ),
    )(
        spectrum,
        land_mask,
        depth_class,
        upwind_signs,
        group_speed,
        speed_ratio,
        mixing,
        growth.reshape(1, bins),
        wind_speed,
        water_depth,
        currents,
        jnp.asarray(trig_table()),
        jnp.asarray(stress_matrix()),
    )


def fits(n, nb, nx, ny, rows):
    return (
        n & (n - 1) == 0
        and rows == 1
        and nx % GROUP == 0
        and nb % GROUP == 0
        and nb % NFREQ == 0
        and ny % (CHUNKS * LANES) == 0
    )


def on_device(*arrays):
    n = lax.axis_size("bin")
    nb, nx, ny = arrays[0].shape
    if fits(n, nb, nx, ny, arrays[-1].shape[1]):
        return fused(n, *arrays)
    return local(*arrays)


def solution(mesh):
    in_specs = (
        P(("ens", "bin"), None, None),
        P(),
        P(),
        P(),
        P(),
        P(),
        P(),
        P(),
        P("ens", None),
        P(),
        P("ens", "bin", None),
    )
    out_specs = (P(("ens", "bin"), None, None), P("ens", "bin", None))
    return jax.shard_map(on_device, mesh=mesh, in_specs=in_specs, out_specs=out_specs, check_vma=False)
```

```python
import functools
import math

import jax
import jax.numpy as jnp
import numpy as np
from jax import lax
from jax.experimental import pallas as pl
from jax.experimental.pallas import tpu as pltpu
from jax.sharding import PartitionSpec as P

NDIR = 32
NFREQ = 24
NCLASS = 8
SUBS = 8


STRESS_SCALE = 0.0625


def extended(shard, sides, width):
    for axis, dim in sides:
        peers, length = (lax.axis_size(axis), shard.shape[dim])
        up = [(i, (i + 1) % peers) for i in range(peers - 1)]
        down = [(j, i) for i, j in up]
        last = lax.slice_in_dim(shard, length - width, length, axis=dim)
        initial = lax.slice_in_dim(shard, 0, width, axis=dim)
        before = lax.ppermute(last, axis, up)
        after = lax.ppermute(initial, axis, down)
        shard = jnp.concatenate([before, shard, after], axis=dim)
    return shard


def angle_of(direction):
    return 2.0 * math.pi * (direction + 0.5) / NDIR


def from_lower(field, axis):
    width = [(0, 0)] * field.ndim
    width[axis] = (1, 0)
    padded = jnp.pad(field, width)
    return lax.slice_in_dim(padded, 0, field.shape[axis], axis=axis)


def from_upper(field, axis):
    width = [(0, 0)] * field.ndim
    width[axis] = (0, 1)
    padded = jnp.pad(field, width)
    return lax.slice_in_dim(padded, 1, field.shape[axis] + 1, axis=axis)


def upwind_step(energy, celerity, cos_abs, sin_abs, sign_x, sign_y, maskf):
    axis_x = energy.ndim - 2
    axis_y = energy.ndim - 1
    flux_x = maskf * (sign_x * celerity * cos_abs * energy)
    flux_y = maskf * (sign_y * celerity * sin_abs * energy)
    diff_x = jnp.where(
        sign_x > 0, flux_x - from_lower(flux_x, axis_x), from_upper(flux_x, axis_x) - flux_x
    )
    diff_y = jnp.where(
        sign_y > 0, flux_y - from_lower(flux_y, axis_y), from_upper(flux_y, axis_y) - flux_y
    )
    return maskf * (energy - diff_x - diff_y)


def integrate(energy, mixing, growth, wind_flat):
    for substep in range(SUBS):
        rounded = energy.astype(jnp.bfloat16)
        energy = (
            energy
            + jnp.dot(mixing, rounded, preferred_element_type=jnp.float32)
            + growth[:, None] * wind_flat[None, :] * energy
        )
    return energy.astype(jnp.bfloat16)


def radiation(fresh, ratio_map):
    energy = fresh.astype(jnp.float32).reshape(NDIR, NFREQ, -1)
    theta = angle_of(jnp.arange(NDIR, dtype=jnp.float32))
    cosine = jnp.cos(theta)
    sine = jnp.sin(theta)
    coeff = jnp.stack([cosine * cosine + 1.0, cosine * sine, sine * sine + 1.0])
    weighted = jnp.einsum("cd,dfn->cfn", coeff, energy, precision=lax.Precision.HIGHEST)
    total = jnp.sum(energy, axis=(0, 1))
    flat_ratio = ratio_map.reshape(NFREQ, -1)
    offset = jnp.array([0.5, 0.0, 0.5], dtype=jnp.float32)
    stress = (
        jnp.sum(flat_ratio[None] * weighted, axis=1) - offset[:, None] * total[None]
    ) * STRESS_SCALE
    return stress.reshape(3, fresh.shape[1], fresh.shape[2])


def forcing(stress_wide, currents, depth_map, maskf):
    slope_x = (stress_wide[:, 2:] - stress_wide[:, :-2]) * 0.5
    inner = stress_wide[:, 1:-1]
    padded_y = jnp.pad(inner, ((0, 0), (0, 0), (1, 1)))
    slope_y = (padded_y[:, :, 2:] - padded_y[:, :, :-2]) * 0.5
    force = jnp.stack([-(slope_x[0] + slope_y[1]), -(slope_x[1] + slope_y[2])])
    return maskf * (currents + force / depth_map)


def local(
    spectrum,
    land_mask,
    depth_class,
    upwind_signs,
    group_speed,
    speed_ratio,
    mixing,
    growth,
    wind_speed,
    water_depth,
    currents,
):
    bin_local = spectrum.shape[0]
    own_rows = currents.shape[1]
    device_index = lax.axis_index("bin")
    bin_ids = device_index * bin_local + jnp.arange(bin_local, dtype=jnp.int32)
    theta = angle_of((bin_ids // NFREQ).astype(jnp.float32))
    cos_abs = jnp.abs(jnp.cos(theta))[:, None, None]
    sin_abs = jnp.abs(jnp.sin(theta))[:, None, None]
    freq_select = (
        (bin_ids % NFREQ)[:, None] == jnp.arange(NFREQ, dtype=jnp.int32)[None, :]
    ).astype(jnp.float32)
    speed_table = jnp.dot(group_speed, freq_select.T, precision=lax.Precision.HIGHEST)
    classes = (depth_class[None] == jnp.arange(NCLASS, dtype=jnp.int32)[:, None, None]).astype(
        jnp.float32
    )
    celerity = jnp.einsum("kb,kxy->bxy", speed_table, classes, precision=lax.Precision.HIGHEST)
    upwind = lax.dynamic_slice_in_dim(upwind_signs, device_index * bin_local, bin_local, 1).astype(
        jnp.float32
    )
    maskf = land_mask.astype(jnp.float32)
    moved = upwind_step(
        spectrum.astype(jnp.float32),
        celerity,
        cos_abs,
        sin_abs,
        upwind[0][:, None, None],
        upwind[1][:, None, None],
        maskf,
    ).astype(jnp.bfloat16)
    first_row = device_index * own_rows
    wind_rows = lax.dynamic_slice_in_dim(wind_speed, first_row, own_rows, 0)
    class_rows = lax.dynamic_slice_in_dim(depth_class, first_row, own_rows, 0)
    mask_own = lax.dynamic_slice_in_dim(maskf, first_row, own_rows, 0)
    ratio_classes = (class_rows[None] == jnp.arange(NCLASS, dtype=jnp.int32)[:, None, None]).astype(
        jnp.float32
    )
    ratio_map = jnp.einsum(
        "kf,kxy->fxy", speed_ratio, ratio_classes, precision=lax.Precision.HIGHEST
    )

    def owner_step(received, wind_block):
        energy = received.astype(jnp.float32).reshape(received.shape[0], -1)
        return integrate(energy, mixing, growth, wind_block.reshape(-1)).reshape(received.shape)

    pieces = [(lax.all_to_all(moved, "bin", split_axis=1, concat_axis=0, tiled=True), wind_rows)]
    fresh = jnp.concatenate([owner_step(piece, wind_part) for piece, wind_part in pieces], axis=2)
    stress = extended(radiation(fresh, ratio_map), (("bin", 1),), 1)
    spectrum_next = lax.all_to_all(fresh, "bin", split_axis=0, concat_axis=1, tiled=True)
    depth_map = jnp.einsum("k,kxy->xy", water_depth, ratio_classes, precision=lax.Precision.HIGHEST)
    return (spectrum_next, forcing(stress, currents, depth_map, mask_own))


CHUNKS = 2
GROUP = 16
LANES = 128
COEF_ROWS = 160
MESH = pl.DeviceIdType.MESH
HIGHEST = lax.Precision.HIGHEST


def flipped(index, k, n):
    result, bit = 0, 1
    while bit < n:
        result = result + ((index // bit + k // bit) % 2) * bit
        bit *= 2
    return result


def stress_matrix():
    theta = angle_of(np.arange(NDIR, dtype=np.float64))
    cosine, sine = np.cos(theta), np.sin(theta)
    weights = np.stack([cosine * cosine + 1.0, cosine * sine, sine * sine + 1.0])
    full = np.repeat(weights, NFREQ, axis=1)
    high = full.astype(jnp.bfloat16).astype(np.float64)
    table = np.ones((8, NDIR * NFREQ), dtype=np.float32)
    table[:3] = high
    table[3:6] = (full - high).astype(jnp.bfloat16)
    return table


def trig_table():
    theta = angle_of(np.arange(NDIR, dtype=np.float64))
    return np.abs(np.stack([np.cos(theta), np.sin(theta)])).astype(np.float32)


def wide(tile, width):
    return jnp.concatenate([tile] * (width // LANES), axis=1)


def fused_kernel(
    n,
    spectrum_hbm,
    mask_hbm,
    class_hbm,
    signs_hbm,
    speed_hbm,
    ratio_hbm,
    mixing_hbm,
    growth_hbm,
    wind_hbm,
    depth_hbm,
    currents_hbm,
    trig_hbm,
    weight_hbm,
    out_hbm,
    currents_out_hbm,
    out_ref,
    currents_out,
    spectrum_v,
    mask_ref,
    class_ref,
    signs_ref,
    speed_ref,
    ratio_ref,
    mixing_v,
    growth_ref,
    wind_ref,
    depth_ref,
    currents_ref,
    trig_ref,
    weight_ref,
    coef_v,
    perm,
    energy_v,
    flux,
    speed_cols,
    sign_cols,
    growth_cols,
    ratio_map,
    send,
    state,
    total,
    back,
    stress,
    halo,
    load_sems,
    store_sems,
    fwd_send,
    fwd_recv,
    ret_send,
    ret_recv,
    halo_send,
    halo_recv,
):
    me = lax.axis_index("bin")
    nb, nx, ny = spectrum_v.shape
    bins = mixing_v.shape[0]
    width = ny // CHUNKS
    groups = nb // GROUP

    loads = [
        pltpu.make_async_copy(src, dst, load_sems.at[i])
        for i, (src, dst) in enumerate(
            [
                (spectrum_hbm, spectrum_v),
                (speed_hbm, speed_ref),
                (signs_hbm, signs_ref),
                (trig_hbm, trig_ref),
                (mask_hbm, mask_ref),
                (class_hbm, class_ref),
                (growth_hbm, growth_ref.at[0]),
                (ratio_hbm, ratio_ref),
                (wind_hbm, wind_ref),
                (mixing_hbm, mixing_v),
                (weight_hbm, weight_ref),
                (depth_hbm, depth_ref),
                (currents_hbm, currents_ref),
            ]
        )
    ]
    for load in loads:
        load.start()
    barrier = pltpu.get_barrier_semaphore()

    def greet(k, carry):
        pl.semaphore_signal(
            barrier, inc=1, device_id={"bin": flipped(me, k, n)}, device_id_type=MESH
        )
        return carry

    lax.fori_loop(1, n, greet, 0)

    for load in loads[1:4]:
        load.wait()
    side = GROUP * nx
    row_id = lax.broadcasted_iota(jnp.int32, (side, side), 0)
    col_id = lax.broadcasted_iota(jnp.int32, (side, side), 1)
    perm[...] = jnp.where(
        (row_id // GROUP == col_id % nx) & (row_id % GROUP == col_id // nx), 1.0, 0.0
    ).astype(jnp.bfloat16)
    spread = jnp.where(
        lax.broadcasted_iota(jnp.int32, (NCLASS, NCLASS * LANES), 0)
        == lax.broadcasted_iota(jnp.int32, (NCLASS, NCLASS * LANES), 1) // LANES,
        1.0,
        0.0,
    )
    columns = lax.dot_general(
        speed_ref[...], spread, (((0,), (0,)), ((), ())), precision=HIGHEST,
        preferred_element_type=jnp.float32,
    )
    columns = jnp.concatenate([columns] * (nb // NFREQ), axis=0)
    for k in range(NCLASS):
        speed_cols[k] = columns[:, k * LANES : (k + 1) * LANES]
    pick = jnp.where(
        lax.broadcasted_iota(jnp.int32, (nb, bins), 1)
        == lax.broadcasted_iota(jnp.int32, (nb, bins), 0) + me * nb,
        1.0,
        0.0,
    ).astype(jnp.bfloat16)
    for axis in range(2):
        signs = jnp.broadcast_to(
            signs_ref[axis : axis + 1, :].astype(jnp.float32), (LANES, bins)
        ).astype(jnp.bfloat16)
        sign_cols[axis] = lax.dot_general(
            pick, signs, (((1,), (1,)), ((), ())), preferred_element_type=jnp.float32
        )
    per_dev = nb // NFREQ
    bin_row = lax.broadcasted_iota(jnp.int32, (nb, LANES), 0)
    for axis in range(2):
        column = jnp.zeros((nb, LANES), jnp.float32)
        for d in range(per_dev):
            column = jnp.where(bin_row // NFREQ == d, trig_ref[axis, me * per_dev + d], column)
        sign_cols[2 + axis] = column

    flux[0] = jnp.zeros((nb, ny), jnp.float32)
    flux[nx + 1] = jnp.zeros((nb, ny), jnp.float32)

    loads[0].wait()
    for g in range(groups):
        block = spectrum_v[g * GROUP : (g + 1) * GROUP].reshape(side, ny)
        turned = jnp.dot(perm[...], block, preferred_element_type=jnp.float32)
        energy_v[:, g * GROUP : (g + 1) * GROUP, :] = turned.astype(jnp.bfloat16).reshape(
            nx, GROUP, ny
        )

    loads[4].wait()
    loads[5].wait()

    def flux_row(i, carry):
        sea = jnp.where(mask_ref[pl.ds(i, 1), :] > 0, class_ref[pl.ds(i, 1), :], -1)
        sea = jnp.broadcast_to(sea, (GROUP, ny))
        for g in range(groups):
            rows = slice(g * GROUP, (g + 1) * GROUP)
            celerity = jnp.zeros((GROUP, ny), jnp.float32)
            for k in range(NCLASS):
                celerity = jnp.where(sea == k, wide(speed_cols[k, rows, :], ny), celerity)
            flux[i + 1, rows, :] = celerity * energy_v[i, rows, :].astype(jnp.float32)
        return carry

    lax.fori_loop(0, nx, flux_row, 0)
    pl.semaphore_wait(barrier, n - 1)

    def forward(c, k):
        return pltpu.make_async_remote_copy(
            src_ref=send.at[c, flipped(me, k, n)],
            dst_ref=state.at[c, 0, pl.ds(pl.multiple_of(me * nb, nb), nb), :],
            send_sem=fwd_send.at[c, k],
            recv_sem=fwd_recv.at[c, k],
            device_id={"bin": flipped(me, k, n)},
            device_id_type=MESH,
        )

    def backward(c, k):
        return pltpu.make_async_remote_copy(
            src_ref=state.at[c, 0, pl.ds(pl.multiple_of(flipped(me, k, n) * nb, nb), nb), :],
            dst_ref=back.at[c, me],
            send_sem=ret_send.at[c, k],
            recv_sem=ret_recv.at[c, k],
            device_id={"bin": flipped(me, k, n)},
            device_id_type=MESH,
        )

    lane = lax.broadcasted_iota(jnp.int32, (GROUP, ny), 1)

    def moved_row(t, carry):
        k = n - 1 - t
        j = flipped(me, k, n)
        maskf = mask_ref[pl.ds(j, 1), :].astype(jnp.float32)
        for g in range(groups):
            rows = slice(g * GROUP, (g + 1) * GROUP)
            sign_x = wide(sign_cols[0, rows, :], ny)
            sign_y = wide(sign_cols[1, rows, :], ny)
            cos_abs = wide(sign_cols[2, rows, :], ny)
            sin_abs = wide(sign_cols[3, rows, :], ny)
            here = flux[j + 1, rows, :]
            lower_y = jnp.where(lane == 0, 0.0, pltpu.roll(here, 1, 1))
            upper_y = jnp.where(lane == ny - 1, 0.0, pltpu.roll(here, ny - 1, 1))
            beside_x = jnp.where(sign_x > 0, flux[j, rows, :], flux[j + 2, rows, :])
            beside_y = jnp.where(sign_y > 0, lower_y, upper_y)
            energy = energy_v[j, rows, :].astype(jnp.float32)
            moved = maskf * (
                energy - cos_abs * (here - beside_x) - sin_abs * (here - beside_y)
            )
            moved = moved.astype(jnp.bfloat16)
            for c in range(CHUNKS):
                send[c, j, rows, :] = moved[:, c * width : (c + 1) * width]

        @pl.when(k > 0)
        def _():
            forward(0, k).start()

        return carry

    lax.fori_loop(0, n, moved_row, 0)
    for c in range(1, CHUNKS):

        def start_forward(t, carry):
            forward(c, n - 1 - t).start()
            return carry

        lax.fori_loop(0, n - 1, start_forward, 0)
    own = pl.ds(pl.multiple_of(me * nb, nb), nb)
    for c in range(CHUNKS):
        state[c, 0, own, :] = send[c, me]

    for load in loads[6:]:
        load.wait()
    growth_cols[...] = jnp.broadcast_to(growth_ref[...], (LANES, bins)).T
    class_row = class_ref[pl.ds(me, 1), :]
    one_hot = jnp.where(
        lax.broadcasted_iota(jnp.int32, (NCLASS, ny), 0)
        == jnp.broadcast_to(class_row, (NCLASS, ny)),
        1.0,
        0.0,
    )
    ratio_map[...] = lax.dot_general(
        ratio_ref[...], one_hot, (((0,), (0,)), ((), ())), precision=HIGHEST,
        preferred_element_type=jnp.float32,
    )
    stress[...] = jnp.zeros_like(stress)
    same_freq = (
        lax.broadcasted_iota(jnp.int32, (NFREQ, bins), 1) % NFREQ
        == lax.broadcasted_iota(jnp.int32, (NFREQ, bins), 0)
    )
    weights = [jnp.where(same_freq, weight_ref[i : i + 1, :], 0.0) for i in range(6)]
    ones = jnp.broadcast_to(weight_ref[6:7, :], (COEF_ROWS - 6 * NFREQ, bins))
    coef_v[...] = jnp.concatenate(weights + [ones], axis=0).astype(jnp.bfloat16)

    @pl.when(me == 0)
    def _():
        halo[0] = jnp.zeros_like(halo[0])

    @pl.when(me == n - 1)
    def _():
        halo[1] = jnp.zeros_like(halo[1])

    tall = 256
    for c in range(CHUNKS):
        lanes = slice(c * width, (c + 1) * width)

        def wait_forward(k, carry):
            forward(c, k).wait_recv()
            return carry

        lax.fori_loop(1, n, wait_forward, 0)
        wind = wind_ref[pl.ds(me, 1), lanes]
        total[...] = state[c, 0].astype(jnp.float32)

        def substep(s, carry):
            now = s % 2
            rounded = state[c, now]
            for r in range(0, bins, tall):
                mixed = jnp.dot(
                    mixing_v[r : r + tall, :], rounded, preferred_element_type=jnp.float32
                )
                held = total[r : r + tall, :]
                held = held + mixed + wide(growth_cols[r : r + tall, :], width) * wind * held
                total[r : r + tall, :] = held
                state[c, 1 - now, r : r + tall, :] = held.astype(jnp.bfloat16)
            return carry

        lax.fori_loop(0, SUBS, substep, 0)

        def start_backward(t, carry):
            backward(c, n - 1 - t).start()
            return carry

        lax.fori_loop(0, n - 1, start_backward, 0)
        back[c, me] = state[c, 0, own, :]
        weighted = jnp.dot(coef_v[...], state[c, 0], preferred_element_type=jnp.float32)
        whole_sum = weighted[6 * NFREQ : 6 * NFREQ + 1, :]
        for comp, offset in enumerate((0.5, 0.0, 0.5)):
            first = comp * NFREQ
            second = (3 + comp) * NFREQ
            part = weighted[first : first + NFREQ, :] + weighted[second : second + NFREQ, :]
            part = jnp.sum(ratio_map[:, lanes] * part, axis=0, keepdims=True)
            stress[comp : comp + 1, lanes] = (part - offset * whole_sum) * STRESS_SCALE

    def to_next():
        return pltpu.make_async_remote_copy(
            src_ref=stress,
            dst_ref=halo.at[0],
            send_sem=halo_send.at[0],
            recv_sem=halo_recv.at[0],
            device_id={"bin": (me + 1) % n},
            device_id_type=MESH,
        )

    def to_previous():
        return pltpu.make_async_remote_copy(
            src_ref=stress,
            dst_ref=halo.at[1],
            send_sem=halo_send.at[1],
            recv_sem=halo_recv.at[1],
            device_id={"bin": (me + n - 1) % n},
            device_id_type=MESH,
        )

    @pl.when(me < n - 1)
    def _():
        to_next().start()

    @pl.when(me > 0)
    def _():
        to_previous().start()

    def store(c):
        lanes = pl.ds(c * width, width)
        return pltpu.make_async_copy(
            out_ref.at[:, :, lanes], out_hbm.at[:, :, lanes], store_sems.at[c]
        )

    def turn_back(c):
        def wait_backward(k, carry):
            backward(c, k).wait_recv()
            return carry

        lax.fori_loop(1, n, wait_backward, 0)
        for g in range(groups):
            block = back[c, :, g * GROUP : (g + 1) * GROUP, :].reshape(side, width)
            turned = lax.dot_general(
                perm[...], block, (((0,), (0,)), ((), ())), preferred_element_type=jnp.float32
            )
            out_ref[g * GROUP : (g + 1) * GROUP, :, c * width : (c + 1) * width] = turned.astype(
                jnp.bfloat16
            ).reshape(GROUP, nx, width)
        store(c).start()

    for c in range(CHUNKS - 1):
        turn_back(c)

    @pl.when(me > 0)
    def _():
        to_next().wait_recv()

    @pl.when(me < n - 1)
    def _():
        to_previous().wait_recv()

    slope_x = (halo[1] - halo[0]) * 0.5
    mine = stress[...]
    lane8 = lax.broadcasted_iota(jnp.int32, mine.shape, 1)
    above = jnp.where(lane8 == ny - 1, 0.0, pltpu.roll(mine, ny - 1, 1))
    below = jnp.where(lane8 == 0, 0.0, pltpu.roll(mine, 1, 1))
    slope_y = (above - below) * 0.5
    depth = jnp.zeros((1, ny), jnp.float32)
    for k in range(NCLASS):
        depth = jnp.where(class_row == k, depth_ref[k], depth)
    sea_row = mask_ref[pl.ds(me, 1), :].astype(jnp.float32)
    for comp in range(2):
        force = -(slope_x[comp : comp + 1, :] + slope_y[comp + 1 : comp + 2, :])
        currents_out[comp] = sea_row * (currents_ref[comp] + force / depth)

    store_currents = pltpu.make_async_copy(
        currents_out, currents_out_hbm, store_sems.at[CHUNKS]
    )
    store_currents.start()
    turn_back(CHUNKS - 1)

    def finish(k, carry):
        for c in range(CHUNKS):
            forward(c, k).wait_send()
            backward(c, k).wait_send()
        return carry

    lax.fori_loop(1, n, finish, 0)

    @pl.when(me < n - 1)
    def _():
        to_next().wait_send()

    @pl.when(me > 0)
    def _():
        to_previous().wait_send()

    store_currents.wait()
    for c in range(CHUNKS):
        store(c).wait()


def fused(
    n,
    spectrum,
    land_mask,
    depth_class,
    upwind_signs,
    group_speed,
    speed_ratio,
    mixing,
    growth,
    wind_speed,
    water_depth,
    currents,
):
    nb, nx, ny = spectrum.shape
    bins = mixing.shape[0]
    width = ny // CHUNKS
    hbm = pl.BlockSpec(memory_space=pltpu.HBM)
    f32, bf16 = jnp.float32, jnp.bfloat16
    dma = pltpu.SemaphoreType.DMA
    return pl.pallas_call(
        functools.partial(fused_kernel, n),
        out_shape=(
            jax.ShapeDtypeStruct(spectrum.shape, bf16),
            jax.ShapeDtypeStruct(currents.shape, f32),
        ),
        in_specs=[hbm] * 13,
        out_specs=(hbm, hbm),
        scratch_shapes=[
            pltpu.VMEM((nb, nx, ny), bf16),
            pltpu.VMEM(currents.shape, f32),
            pltpu.VMEM((nb, nx, ny), bf16),
            pltpu.VMEM(land_mask.shape, jnp.int32),
            pltpu.VMEM(depth_class.shape, jnp.int32),
            pltpu.VMEM(upwind_signs.shape, jnp.int32),
            pltpu.VMEM(group_speed.shape, f32),
            pltpu.VMEM(speed_ratio.shape, f32),
            pltpu.VMEM((bins, bins), bf16),
            pltpu.VMEM((1, bins), f32),
            pltpu.VMEM(wind_speed.shape, f32),
            pltpu.SMEM(water_depth.shape, f32),
            pltpu.VMEM(currents.shape, f32),
            pltpu.SMEM((2, NDIR), f32),
            pltpu.VMEM((8, bins), f32),
            pltpu.VMEM((COEF_ROWS, bins), bf16),
            pltpu.VMEM((GROUP * nx, GROUP * nx), bf16),
            pltpu.VMEM((nx, nb, ny), bf16),
            pltpu.VMEM((nx + 2, nb, ny), f32),
            pltpu.VMEM((NCLASS, nb, LANES), f32),
            pltpu.VMEM((4, nb, LANES), f32),
            pltpu.VMEM((bins, LANES), f32),
            pltpu.VMEM((NFREQ, ny), f32),
            pltpu.VMEM((CHUNKS, nx, nb, width), bf16),
            pltpu.VMEM((CHUNKS, 2, bins, width), bf16),
            pltpu.VMEM((bins, width), f32),
            pltpu.VMEM((CHUNKS, nx, nb, width), bf16),
            pltpu.VMEM((8, ny), f32),
            pltpu.VMEM((2, 8, ny), f32),
            dma((13,)),
            dma((CHUNKS + 1,)),
            dma((CHUNKS, n)),
            dma((CHUNKS, n)),
            dma((CHUNKS, n)),
            dma((CHUNKS, n)),
            dma((2,)),
            dma((2,)),
        ],
        compiler_params=pltpu.CompilerParams(
            collective_id=0, has_side_effects=True, vmem_limit_bytes=64 * 1024 * 1024
        ),
    )(
        spectrum,
        land_mask,
        depth_class,
        upwind_signs,
        group_speed,
        speed_ratio,
        mixing,
        growth,
        wind_speed,
        water_depth,
        currents,
        jnp.asarray(trig_table()),
        jnp.asarray(stress_matrix()),
    )


def hand_on_kernel(*refs):
    sems = refs[-1]
    count = (len(refs) - 1) // 2
    copies = [
        pltpu.make_async_copy(refs[i], refs[count + i], sems.at[i]) for i in range(count)
    ]
    for copy in copies:
        copy.start()
    for copy in copies:
        copy.wait()


def hand_on(*arrays):
    hbm = pl.BlockSpec(memory_space=pltpu.HBM)
    return pl.pallas_call(
        hand_on_kernel,
        out_shape=tuple(jax.ShapeDtypeStruct(a.shape, a.dtype) for a in arrays),
        in_specs=[hbm] * len(arrays),
        out_specs=tuple([hbm] * len(arrays)),
        scratch_shapes=[pltpu.SemaphoreType.DMA((len(arrays),))],
        compiler_params=pltpu.CompilerParams(vmem_limit_bytes=64 * 1024 * 1024),
    )(*arrays)


def fits(n, nb, nx, ny, rows):
    return (
        n & (n - 1) == 0
        and rows == 1
        and nx % GROUP == 0
        and nb % GROUP == 0
        and nb % NFREQ == 0
        and ny % (CHUNKS * LANES) == 0
    )


def on_device(*arrays):
    n = lax.axis_size("bin")
    nb, nx, ny = arrays[0].shape
    if fits(n, nb, nx, ny, arrays[-1].shape[1]):
        return hand_on(*fused(n, *arrays))
    return local(*arrays)


def solution(mesh):
    in_specs = (
        P(("ens", "bin"), None, None),
        P(),
        P(),
        P(),
        P(),
        P(),
        P(),
        P(),
        P("ens", None),
        P(),
        P("ens", "bin", None),
    )
    out_specs = (P(("ens", "bin"), None, None), P("ens", "bin", None))
    return jax.shard_map(on_device, mesh=mesh, in_specs=in_specs, out_specs=out_specs, check_vma=False)
```

```python
import functools
import math

import jax
import jax.numpy as jnp
import numpy as np
from jax import lax
from jax.experimental import pallas as pl
from jax.experimental.pallas import tpu as pltpu
from jax.sharding import PartitionSpec as P

NDIR = 32
NFREQ = 24
NCLASS = 8
SUBS = 8


STRESS_SCALE = 0.0625


def extended(shard, sides, width):
    for axis, dim in sides:
        peers, length = (lax.axis_size(axis), shard.shape[dim])
        up = [(i, (i + 1) % peers) for i in range(peers - 1)]
        down = [(j, i) for i, j in up]
        last = lax.slice_in_dim(shard, length - width, length, axis=dim)
        initial = lax.slice_in_dim(shard, 0, width, axis=dim)
        before = lax.ppermute(last, axis, up)
        after = lax.ppermute(initial, axis, down)
        shard = jnp.concatenate([before, shard, after], axis=dim)
    return shard


def angle_of(direction):
    return 2.0 * math.pi * (direction + 0.5) / NDIR


def from_lower(field, axis):
    width = [(0, 0)] * field.ndim
    width[axis] = (1, 0)
    padded = jnp.pad(field, width)
    return lax.slice_in_dim(padded, 0, field.shape[axis], axis=axis)


def from_upper(field, axis):
    width = [(0, 0)] * field.ndim
    width[axis] = (0, 1)
    padded = jnp.pad(field, width)
    return lax.slice_in_dim(padded, 1, field.shape[axis] + 1, axis=axis)


def upwind_step(energy, celerity, cos_abs, sin_abs, sign_x, sign_y, maskf):
    axis_x = energy.ndim - 2
    axis_y = energy.ndim - 1
    flux_x = maskf * (sign_x * celerity * cos_abs * energy)
    flux_y = maskf * (sign_y * celerity * sin_abs * energy)
    diff_x = jnp.where(
        sign_x > 0, flux_x - from_lower(flux_x, axis_x), from_upper(flux_x, axis_x) - flux_x
    )
    diff_y = jnp.where(
        sign_y > 0, flux_y - from_lower(flux_y, axis_y), from_upper(flux_y, axis_y) - flux_y
    )
    return maskf * (energy - diff_x - diff_y)


def integrate(energy, mixing, growth, wind_flat):
    for substep in range(SUBS):
        rounded = energy.astype(jnp.bfloat16)
        energy = (
            energy
            + jnp.dot(mixing, rounded, preferred_element_type=jnp.float32)
            + growth[:, None] * wind_flat[None, :] * energy
        )
    return energy.astype(jnp.bfloat16)


def radiation(fresh, ratio_map):
    energy = fresh.astype(jnp.float32).reshape(NDIR, NFREQ, -1)
    theta = angle_of(jnp.arange(NDIR, dtype=jnp.float32))
    cosine = jnp.cos(theta)
    sine = jnp.sin(theta)
    coeff = jnp.stack([cosine * cosine + 1.0, cosine * sine, sine * sine + 1.0])
    weighted = jnp.einsum("cd,dfn->cfn", coeff, energy, precision=lax.Precision.HIGHEST)
    total = jnp.sum(energy, axis=(0, 1))
    flat_ratio = ratio_map.reshape(NFREQ, -1)
    offset = jnp.array([0.5, 0.0, 0.5], dtype=jnp.float32)
    stress = (
        jnp.sum(flat_ratio[None] * weighted, axis=1) - offset[:, None] * total[None]
    ) * STRESS_SCALE
    return stress.reshape(3, fresh.shape[1], fresh.shape[2])


def forcing(stress_wide, currents, depth_map, maskf):
    slope_x = (stress_wide[:, 2:] - stress_wide[:, :-2]) * 0.5
    inner = stress_wide[:, 1:-1]
    padded_y = jnp.pad(inner, ((0, 0), (0, 0), (1, 1)))
    slope_y = (padded_y[:, :, 2:] - padded_y[:, :, :-2]) * 0.5
    force = jnp.stack([-(slope_x[0] + slope_y[1]), -(slope_x[1] + slope_y[2])])
    return maskf * (currents + force / depth_map)


def local(
    spectrum,
    land_mask,
    depth_class,
    upwind_signs,
    group_speed,
    speed_ratio,
    mixing,
    growth,
    wind_speed,
    water_depth,
    currents,
):
    bin_local = spectrum.shape[0]
    own_rows = currents.shape[1]
    device_index = lax.axis_index("bin")
    bin_ids = device_index * bin_local + jnp.arange(bin_local, dtype=jnp.int32)
    theta = angle_of((bin_ids // NFREQ).astype(jnp.float32))
    cos_abs = jnp.abs(jnp.cos(theta))[:, None, None]
    sin_abs = jnp.abs(jnp.sin(theta))[:, None, None]
    freq_select = (
        (bin_ids % NFREQ)[:, None] == jnp.arange(NFREQ, dtype=jnp.int32)[None, :]
    ).astype(jnp.float32)
    speed_table = jnp.dot(group_speed, freq_select.T, precision=lax.Precision.HIGHEST)
    classes = (depth_class[None] == jnp.arange(NCLASS, dtype=jnp.int32)[:, None, None]).astype(
        jnp.float32
    )
    celerity = jnp.einsum("kb,kxy->bxy", speed_table, classes, precision=lax.Precision.HIGHEST)
    upwind = lax.dynamic_slice_in_dim(upwind_signs, device_index * bin_local, bin_local, 1).astype(
        jnp.float32
    )
    maskf = land_mask.astype(jnp.float32)
    moved = upwind_step(
        spectrum.astype(jnp.float32),
        celerity,
        cos_abs,
        sin_abs,
        upwind[0][:, None, None],
        upwind[1][:, None, None],
        maskf,
    ).astype(jnp.bfloat16)
    first_row = device_index * own_rows
    wind_rows = lax.dynamic_slice_in_dim(wind_speed, first_row, own_rows, 0)
    class_rows = lax.dynamic_slice_in_dim(depth_class, first_row, own_rows, 0)
    mask_own = lax.dynamic_slice_in_dim(maskf, first_row, own_rows, 0)
    ratio_classes = (class_rows[None] == jnp.arange(NCLASS, dtype=jnp.int32)[:, None, None]).astype(
        jnp.float32
    )
    ratio_map = jnp.einsum(
        "kf,kxy->fxy", speed_ratio, ratio_classes, precision=lax.Precision.HIGHEST
    )

    def owner_step(received, wind_block):
        energy = received.astype(jnp.float32).reshape(received.shape[0], -1)
        return integrate(energy, mixing, growth, wind_block.reshape(-1)).reshape(received.shape)

    pieces = [(lax.all_to_all(moved, "bin", split_axis=1, concat_axis=0, tiled=True), wind_rows)]
    fresh = jnp.concatenate([owner_step(piece, wind_part) for piece, wind_part in pieces], axis=2)
    stress = extended(radiation(fresh, ratio_map), (("bin", 1),), 1)
    spectrum_next = lax.all_to_all(fresh, "bin", split_axis=0, concat_axis=1, tiled=True)
    depth_map = jnp.einsum("k,kxy->xy", water_depth, ratio_classes, precision=lax.Precision.HIGHEST)
    return (spectrum_next, forcing(stress, currents, depth_map, mask_own))


CHUNKS = 2
GROUP = 16
LANES = 128
COEF_ROWS = 160
MESH = pl.DeviceIdType.MESH
HIGHEST = lax.Precision.HIGHEST


def flipped(index, k, n):
    result, bit = 0, 1
    while bit < n:
        result = result + ((index // bit + k // bit) % 2) * bit
        bit *= 2
    return result


def stress_matrix():
    theta = angle_of(np.arange(NDIR, dtype=np.float64))
    cosine, sine = np.cos(theta), np.sin(theta)
    weights = np.stack([cosine * cosine + 1.0, cosine * sine, sine * sine + 1.0])
    full = np.repeat(weights, NFREQ, axis=1)
    high = full.astype(jnp.bfloat16).astype(np.float64)
    table = np.ones((8, NDIR * NFREQ), dtype=np.float32)
    table[:3] = high
    table[3:6] = (full - high).astype(jnp.bfloat16)
    return table


def trig_table():
    theta = angle_of(np.arange(NDIR, dtype=np.float64))
    return np.abs(np.stack([np.cos(theta), np.sin(theta)])).astype(np.float32)


def turning(outer, inner):
    side = outer * inner
    row_id = lax.broadcasted_iota(jnp.int32, (side, side), 0)
    col_id = lax.broadcasted_iota(jnp.int32, (side, side), 1)
    hit = (row_id // inner == col_id % outer) & (row_id % inner == col_id // outer)
    return jnp.where(hit, 1.0, 0.0).astype(jnp.bfloat16)


def wide(tile, width):
    return jnp.concatenate([tile] * (width // LANES), axis=1)


def fused_kernel(
    n,
    spectrum_hbm,
    mask_hbm,
    class_hbm,
    signs_hbm,
    speed_hbm,
    ratio_hbm,
    mixing_hbm,
    growth_hbm,
    wind_hbm,
    depth_hbm,
    currents_hbm,
    trig_hbm,
    weight_hbm,
    back,
    currents_out_hbm,
    currents_out,
    spectrum_v,
    mask_ref,
    class_ref,
    signs_ref,
    speed_ref,
    ratio_ref,
    mixing_v,
    growth_ref,
    wind_ref,
    depth_ref,
    currents_ref,
    trig_ref,
    weight_ref,
    coef_v,
    perm,
    energy_v,
    flux,
    speed_cols,
    sign_cols,
    growth_cols,
    ratio_map,
    send,
    state,
    total,
    stress,
    halo,
    load_sems,
    store_sems,
    fwd_send,
    fwd_recv,
    ret_send,
    ret_recv,
    halo_send,
    halo_recv,
):
    me = lax.axis_index("bin")
    nb, nx, ny = spectrum_v.shape
    bins = mixing_v.shape[0]
    width = ny // CHUNKS
    groups = nb // GROUP

    loads = [
        pltpu.make_async_copy(src, dst, load_sems.at[i])
        for i, (src, dst) in enumerate(
            [
                (spectrum_hbm, spectrum_v),
                (speed_hbm, speed_ref),
                (signs_hbm, signs_ref),
                (trig_hbm, trig_ref),
                (mask_hbm, mask_ref),
                (class_hbm, class_ref),
                (growth_hbm, growth_ref.at[0]),
                (ratio_hbm, ratio_ref),
                (wind_hbm, wind_ref),
                (mixing_hbm, mixing_v),
                (weight_hbm, weight_ref),
                (depth_hbm, depth_ref),
                (currents_hbm, currents_ref),
            ]
        )
    ]
    for load in loads:
        load.start()
    barrier = pltpu.get_barrier_semaphore()

    def greet(k, carry):
        pl.semaphore_signal(
            barrier, inc=1, device_id={"bin": flipped(me, k, n)}, device_id_type=MESH
        )
        return carry

    lax.fori_loop(1, n, greet, 0)

    for load in loads[1:4]:
        load.wait()
    side = GROUP * nx
    perm[...] = turning(nx, GROUP)
    spread = jnp.where(
        lax.broadcasted_iota(jnp.int32, (NCLASS, NCLASS * LANES), 0)
        == lax.broadcasted_iota(jnp.int32, (NCLASS, NCLASS * LANES), 1) // LANES,
        1.0,
        0.0,
    )
    columns = lax.dot_general(
        speed_ref[...], spread, (((0,), (0,)), ((), ())), precision=HIGHEST,
        preferred_element_type=jnp.float32,
    )
    columns = jnp.concatenate([columns] * (nb // NFREQ), axis=0)
    for k in range(NCLASS):
        speed_cols[k] = columns[:, k * LANES : (k + 1) * LANES]
    pick = jnp.where(
        lax.broadcasted_iota(jnp.int32, (nb, bins), 1)
        == lax.broadcasted_iota(jnp.int32, (nb, bins), 0) + me * nb,
        1.0,
        0.0,
    ).astype(jnp.bfloat16)
    for axis in range(2):
        signs = jnp.broadcast_to(
            signs_ref[axis : axis + 1, :].astype(jnp.float32), (LANES, bins)
        ).astype(jnp.bfloat16)
        sign_cols[axis] = lax.dot_general(
            pick, signs, (((1,), (1,)), ((), ())), preferred_element_type=jnp.float32
        )
    per_dev = nb // NFREQ
    bin_row = lax.broadcasted_iota(jnp.int32, (nb, LANES), 0)
    for axis in range(2):
        column = jnp.zeros((nb, LANES), jnp.float32)
        for d in range(per_dev):
            column = jnp.where(bin_row // NFREQ == d, trig_ref[axis, me * per_dev + d], column)
        sign_cols[2 + axis] = column

    flux[0] = jnp.zeros((nb, ny), jnp.float32)
    flux[nx + 1] = jnp.zeros((nb, ny), jnp.float32)

    loads[0].wait()
    for g in range(groups):
        block = spectrum_v[g * GROUP : (g + 1) * GROUP].reshape(side, ny)
        turned = jnp.dot(perm[...], block, preferred_element_type=jnp.float32)
        energy_v[:, g * GROUP : (g + 1) * GROUP, :] = turned.astype(jnp.bfloat16).reshape(
            nx, GROUP, ny
        )

    loads[4].wait()
    loads[5].wait()

    def flux_row(i, carry):
        sea = jnp.where(mask_ref[pl.ds(i, 1), :] > 0, class_ref[pl.ds(i, 1), :], -1)
        sea = jnp.broadcast_to(sea, (GROUP, ny))
        for g in range(groups):
            rows = slice(g * GROUP, (g + 1) * GROUP)
            celerity = jnp.zeros((GROUP, ny), jnp.float32)
            for k in range(NCLASS):
                celerity = jnp.where(sea == k, wide(speed_cols[k, rows, :], ny), celerity)
            flux[i + 1, rows, :] = celerity * energy_v[i, rows, :].astype(jnp.float32)
        return carry

    lax.fori_loop(0, nx, flux_row, 0)
    pl.semaphore_wait(barrier, n - 1)

    def forward(c, k):
        return pltpu.make_async_remote_copy(
            src_ref=send.at[c, flipped(me, k, n)],
            dst_ref=state.at[c, 0, pl.ds(pl.multiple_of(me * nb, nb), nb), :],
            send_sem=fwd_send.at[c, k],
            recv_sem=fwd_recv.at[c, k],
            device_id={"bin": flipped(me, k, n)},
            device_id_type=MESH,
        )

    def backward(c, k):
        return pltpu.make_async_remote_copy(
            src_ref=state.at[c, 0, pl.ds(pl.multiple_of(flipped(me, k, n) * nb, nb), nb), :],
            dst_ref=back.at[c, me],
            send_sem=ret_send.at[c, k],
            recv_sem=ret_recv.at[c, k],
            device_id={"bin": flipped(me, k, n)},
            device_id_type=MESH,
        )

    def keep(c):
        return pltpu.make_async_copy(
            state.at[c, 0, pl.ds(pl.multiple_of(me * nb, nb), nb), :],
            back.at[c, me],
            store_sems.at[c],
        )

    lane = lax.broadcasted_iota(jnp.int32, (GROUP, ny), 1)

    def moved_row(t, carry):
        k = n - 1 - t
        j = flipped(me, k, n)
        maskf = mask_ref[pl.ds(j, 1), :].astype(jnp.float32)
        for g in range(groups):
            rows = slice(g * GROUP, (g + 1) * GROUP)
            sign_x = wide(sign_cols[0, rows, :], ny)
            sign_y = wide(sign_cols[1, rows, :], ny)
            cos_abs = wide(sign_cols[2, rows, :], ny)
            sin_abs = wide(sign_cols[3, rows, :], ny)
            here = flux[j + 1, rows, :]
            lower_y = jnp.where(lane == 0, 0.0, pltpu.roll(here, 1, 1))
            upper_y = jnp.where(lane == ny - 1, 0.0, pltpu.roll(here, ny - 1, 1))
            beside_x = jnp.where(sign_x > 0, flux[j, rows, :], flux[j + 2, rows, :])
            beside_y = jnp.where(sign_y > 0, lower_y, upper_y)
            energy = energy_v[j, rows, :].astype(jnp.float32)
            moved = maskf * (
                energy - cos_abs * (here - beside_x) - sin_abs * (here - beside_y)
            )
            moved = moved.astype(jnp.bfloat16)
            for c in range(CHUNKS):
                send[c, j, rows, :] = moved[:, c * width : (c + 1) * width]

        @pl.when(k > 0)
        def _():
            forward(0, k).start()

        return carry

    lax.fori_loop(0, n, moved_row, 0)
    for c in range(1, CHUNKS):

        def start_forward(t, carry):
            forward(c, n - 1 - t).start()
            return carry

        lax.fori_loop(0, n - 1, start_forward, 0)
    own = pl.ds(pl.multiple_of(me * nb, nb), nb)
    for c in range(CHUNKS):
        state[c, 0, own, :] = send[c, me]

    for load in loads[6:]:
        load.wait()
    growth_cols[...] = jnp.broadcast_to(growth_ref[...], (LANES, bins)).T
    class_row = class_ref[pl.ds(me, 1), :]
    one_hot = jnp.where(
        lax.broadcasted_iota(jnp.int32, (NCLASS, ny), 0)
        == jnp.broadcast_to(class_row, (NCLASS, ny)),
        1.0,
        0.0,
    )
    ratio_map[...] = lax.dot_general(
        ratio_ref[...], one_hot, (((0,), (0,)), ((), ())), precision=HIGHEST,
        preferred_element_type=jnp.float32,
    )
    stress[...] = jnp.zeros_like(stress)
    same_freq = (
        lax.broadcasted_iota(jnp.int32, (NFREQ, bins), 1) % NFREQ
        == lax.broadcasted_iota(jnp.int32, (NFREQ, bins), 0)
    )
    weights = [jnp.where(same_freq, weight_ref[i : i + 1, :], 0.0) for i in range(6)]
    ones = jnp.broadcast_to(weight_ref[6:7, :], (COEF_ROWS - 6 * NFREQ, bins))
    coef_v[...] = jnp.concatenate(weights + [ones], axis=0).astype(jnp.bfloat16)

    @pl.when(me == 0)
    def _():
        halo[0] = jnp.zeros_like(halo[0])

    @pl.when(me == n - 1)
    def _():
        halo[1] = jnp.zeros_like(halo[1])

    tall = 256
    for c in range(CHUNKS):
        lanes = slice(c * width, (c + 1) * width)

        def wait_forward(k, carry):
            forward(c, k).wait_recv()
            return carry

        lax.fori_loop(1, n, wait_forward, 0)
        wind = wind_ref[pl.ds(me, 1), lanes]
        total[...] = state[c, 0].astype(jnp.float32)

        def substep(s, carry):
            now = s % 2
            rounded = state[c, now]
            for r in range(0, bins, tall):
                mixed = jnp.dot(
                    mixing_v[r : r + tall, :], rounded, preferred_element_type=jnp.float32
                )
                held = total[r : r + tall, :]
                held = held + mixed + wide(growth_cols[r : r + tall, :], width) * wind * held
                total[r : r + tall, :] = held
                state[c, 1 - now, r : r + tall, :] = held.astype(jnp.bfloat16)
            return carry

        lax.fori_loop(0, SUBS, substep, 0)

        def start_backward(t, carry):
            backward(c, n - 1 - t).start()
            return carry

        lax.fori_loop(0, n - 1, start_backward, 0)
        keep(c).start()
        weighted = jnp.dot(coef_v[...], state[c, 0], preferred_element_type=jnp.float32)
        whole_sum = weighted[6 * NFREQ : 6 * NFREQ + 1, :]
        for comp, offset in enumerate((0.5, 0.0, 0.5)):
            first = comp * NFREQ
            second = (3 + comp) * NFREQ
            part = weighted[first : first + NFREQ, :] + weighted[second : second + NFREQ, :]
            part = jnp.sum(ratio_map[:, lanes] * part, axis=0, keepdims=True)
            stress[comp : comp + 1, lanes] = (part - offset * whole_sum) * STRESS_SCALE

    def to_next():
        return pltpu.make_async_remote_copy(
            src_ref=stress,
            dst_ref=halo.at[0],
            send_sem=halo_send.at[0],
            recv_sem=halo_recv.at[0],
            device_id={"bin": (me + 1) % n},
            device_id_type=MESH,
        )

    def to_previous():
        return pltpu.make_async_remote_copy(
            src_ref=stress,
            dst_ref=halo.at[1],
            send_sem=halo_send.at[1],
            recv_sem=halo_recv.at[1],
            device_id={"bin": (me + n - 1) % n},
            device_id_type=MESH,
        )

    @pl.when(me < n - 1)
    def _():
        to_next().start()

    @pl.when(me > 0)
    def _():
        to_previous().start()

    @pl.when(me > 0)
    def _():
        to_next().wait_recv()

    @pl.when(me < n - 1)
    def _():
        to_previous().wait_recv()

    slope_x = (halo[1] - halo[0]) * 0.5
    mine = stress[...]
    lane8 = lax.broadcasted_iota(jnp.int32, mine.shape, 1)
    above = jnp.where(lane8 == ny - 1, 0.0, pltpu.roll(mine, ny - 1, 1))
    below = jnp.where(lane8 == 0, 0.0, pltpu.roll(mine, 1, 1))
    slope_y = (above - below) * 0.5
    depth = jnp.zeros((1, ny), jnp.float32)
    for k in range(NCLASS):
        depth = jnp.where(class_row == k, depth_ref[k], depth)
    sea_row = mask_ref[pl.ds(me, 1), :].astype(jnp.float32)
    for comp in range(2):
        force = -(slope_x[comp : comp + 1, :] + slope_y[comp + 1 : comp + 2, :])
        currents_out[comp] = sea_row * (currents_ref[comp] + force / depth)

    store_currents = pltpu.make_async_copy(
        currents_out, currents_out_hbm, store_sems.at[CHUNKS]
    )
    store_currents.start()

    def wait_backward(k, carry):
        for c in range(CHUNKS):
            backward(c, k).wait_recv()
        return carry

    lax.fori_loop(1, n, wait_backward, 0)

    def finish(k, carry):
        for c in range(CHUNKS):
            forward(c, k).wait_send()
            backward(c, k).wait_send()
        return carry

    lax.fori_loop(1, n, finish, 0)

    @pl.when(me < n - 1)
    def _():
        to_next().wait_send()

    @pl.when(me > 0)
    def _():
        to_previous().wait_send()

    store_currents.wait()
    for c in range(CHUNKS):
        keep(c).wait()


def fused(
    n,
    spectrum,
    land_mask,
    depth_class,
    upwind_signs,
    group_speed,
    speed_ratio,
    mixing,
    growth,
    wind_speed,
    water_depth,
    currents,
):
    nb, nx, ny = spectrum.shape
    bins = mixing.shape[0]
    width = ny // CHUNKS
    hbm = pl.BlockSpec(memory_space=pltpu.HBM)
    f32, bf16 = jnp.float32, jnp.bfloat16
    dma = pltpu.SemaphoreType.DMA
    return pl.pallas_call(
        functools.partial(fused_kernel, n),
        out_shape=(
            jax.ShapeDtypeStruct((CHUNKS, nx, nb, width), bf16),
            jax.ShapeDtypeStruct(currents.shape, f32),
        ),
        in_specs=[hbm] * 13,
        out_specs=(hbm, hbm),
        scratch_shapes=[
            pltpu.VMEM(currents.shape, f32),
            pltpu.VMEM((nb, nx, ny), bf16),
            pltpu.VMEM(land_mask.shape, jnp.int32),
            pltpu.VMEM(depth_class.shape, jnp.int32),
            pltpu.VMEM(upwind_signs.shape, jnp.int32),
            pltpu.VMEM(group_speed.shape, f32),
            pltpu.VMEM(speed_ratio.shape, f32),
            pltpu.VMEM((bins, bins), bf16),
            pltpu.VMEM((1, bins), f32),
            pltpu.VMEM(wind_speed.shape, f32),
            pltpu.SMEM(water_depth.shape, f32),
            pltpu.VMEM(currents.shape, f32),
            pltpu.SMEM((2, NDIR), f32),
            pltpu.VMEM((8, bins), f32),
            pltpu.VMEM((COEF_ROWS, bins), bf16),
            pltpu.VMEM((GROUP * nx, GROUP * nx), bf16),
            pltpu.VMEM((nx, nb, ny), bf16),
            pltpu.VMEM((nx + 2, nb, ny), f32),
            pltpu.VMEM((NCLASS, nb, LANES), f32),
            pltpu.VMEM((4, nb, LANES), f32),
            pltpu.VMEM((bins, LANES), f32),
            pltpu.VMEM((NFREQ, ny), f32),
            pltpu.VMEM((CHUNKS, nx, nb, width), bf16),
            pltpu.VMEM((CHUNKS, 2, bins, width), bf16),
            pltpu.VMEM((bins, width), f32),
            pltpu.VMEM((8, ny), f32),
            pltpu.VMEM((2, 8, ny), f32),
            dma((13,)),
            dma((CHUNKS + 1,)),
            dma((CHUNKS, n)),
            dma((CHUNKS, n)),
            dma((CHUNKS, n)),
            dma((CHUNKS, n)),
            dma((2,)),
            dma((2,)),
        ],
        compiler_params=pltpu.CompilerParams(
            collective_id=0, has_side_effects=True, vmem_limit_bytes=64 * 1024 * 1024
        ),
    )(
        spectrum,
        land_mask,
        depth_class,
        upwind_signs,
        group_speed,
        speed_ratio,
        mixing,
        growth,
        wind_speed,
        water_depth,
        currents,
        jnp.asarray(trig_table()),
        jnp.asarray(stress_matrix()),
    )


def turn_kernel(back, currents_in, fresh_out, currents_out, back_v, fresh_v, currents_v, sems):
    chunks, nx, nb, width = back_v.shape
    groups = [pl.ds(g, GROUP) for g in range(0, nb, GROUP)]
    loads = [pltpu.make_async_copy(back.at[c], back_v.at[c], sems.at[0, c]) for c in range(chunks)]
    stores = [
        pltpu.make_async_copy(fresh_v.at[g], fresh_out.at[g], sems.at[1, i])
        for i, g in enumerate(groups)
    ]
    load_currents = pltpu.make_async_copy(currents_in, currents_v, sems.at[0, chunks])
    store_currents = pltpu.make_async_copy(currents_v, currents_out, sems.at[1, len(groups)])
    for load in loads:
        load.start()
    load_currents.start()
    perm = turning(GROUP, nx)
    load_currents.wait()
    store_currents.start()
    for load in loads:
        load.wait()
    for g, store in zip(groups, stores):
        for c in range(chunks):
            block = back_v[c, :, g, :].reshape(nx * GROUP, width)
            turned = jnp.dot(perm, block, preferred_element_type=jnp.float32)
            fresh_v[g, :, c * width : (c + 1) * width] = turned.astype(jnp.bfloat16).reshape(
                GROUP, nx, width
            )
        store.start()
    for store in stores + [store_currents]:
        store.wait()


def turn(back, currents):
    chunks, nx, nb, width = back.shape
    hbm = pl.BlockSpec(memory_space=pltpu.HBM)
    fresh = jax.ShapeDtypeStruct((nb, nx, chunks * width), back.dtype)
    count = max(chunks, nb // GROUP) + 1
    return pl.pallas_call(
        turn_kernel,
        out_shape=(fresh, jax.ShapeDtypeStruct(currents.shape, currents.dtype)),
        in_specs=[hbm, hbm],
        out_specs=(hbm, hbm),
        scratch_shapes=[
            pltpu.VMEM(back.shape, back.dtype),
            pltpu.VMEM(fresh.shape, fresh.dtype),
            pltpu.VMEM(currents.shape, currents.dtype),
            pltpu.SemaphoreType.DMA((2, count)),
        ],
        compiler_params=pltpu.CompilerParams(vmem_limit_bytes=64 * 1024 * 1024),
    )(back, currents)


def fits(n, nb, nx, ny, rows):
    return (
        n & (n - 1) == 0
        and rows == 1
        and nx % GROUP == 0
        and nb % GROUP == 0
        and nb % NFREQ == 0
        and ny % (CHUNKS * LANES) == 0
    )


def on_device(*arrays):
    n = lax.axis_size("bin")
    nb, nx, ny = arrays[0].shape
    if fits(n, nb, nx, ny, arrays[-1].shape[1]):
        return turn(*fused(n, *arrays))
    return local(*arrays)


def solution(mesh):
    in_specs = (
        P(("ens", "bin"), None, None),
        P(),
        P(),
        P(),
        P(),
        P(),
        P(),
        P(),
        P("ens", None),
        P(),
        P("ens", "bin", None),
    )
    out_specs = (P(("ens", "bin"), None, None), P("ens", "bin", None))
    return jax.shard_map(on_device, mesh=mesh, in_specs=in_specs, out_specs=out_specs, check_vma=False)
```

```python
import functools
import math

import jax
import jax.numpy as jnp
import numpy as np
from jax import lax
from jax.experimental import pallas as pl
from jax.experimental.pallas import tpu as pltpu
from jax.sharding import PartitionSpec as P

NDIR = 32
NFREQ = 24
NCLASS = 8
SUBS = 8


STRESS_SCALE = 0.0625


def extended(shard, sides, width):
    for axis, dim in sides:
        peers, length = (lax.axis_size(axis), shard.shape[dim])
        up = [(i, (i + 1) % peers) for i in range(peers - 1)]
        down = [(j, i) for i, j in up]
        last = lax.slice_in_dim(shard, length - width, length, axis=dim)
        initial = lax.slice_in_dim(shard, 0, width, axis=dim)
        before = lax.ppermute(last, axis, up)
        after = lax.ppermute(initial, axis, down)
        shard = jnp.concatenate([before, shard, after], axis=dim)
    return shard


def angle_of(direction):
    return 2.0 * math.pi * (direction + 0.5) / NDIR


def from_lower(field, axis):
    width = [(0, 0)] * field.ndim
    width[axis] = (1, 0)
    padded = jnp.pad(field, width)
    return lax.slice_in_dim(padded, 0, field.shape[axis], axis=axis)


def from_upper(field, axis):
    width = [(0, 0)] * field.ndim
    width[axis] = (0, 1)
    padded = jnp.pad(field, width)
    return lax.slice_in_dim(padded, 1, field.shape[axis] + 1, axis=axis)


def upwind_step(energy, celerity, cos_abs, sin_abs, sign_x, sign_y, maskf):
    axis_x = energy.ndim - 2
    axis_y = energy.ndim - 1
    flux_x = maskf * (sign_x * celerity * cos_abs * energy)
    flux_y = maskf * (sign_y * celerity * sin_abs * energy)
    diff_x = jnp.where(
        sign_x > 0, flux_x - from_lower(flux_x, axis_x), from_upper(flux_x, axis_x) - flux_x
    )
    diff_y = jnp.where(
        sign_y > 0, flux_y - from_lower(flux_y, axis_y), from_upper(flux_y, axis_y) - flux_y
    )
    return maskf * (energy - diff_x - diff_y)


def integrate(energy, mixing, growth, wind_flat):
    for substep in range(SUBS):
        rounded = energy.astype(jnp.bfloat16)
        energy = (
            energy
            + jnp.dot(mixing, rounded, preferred_element_type=jnp.float32)
            + growth[:, None] * wind_flat[None, :] * energy
        )
    return energy.astype(jnp.bfloat16)


def radiation(fresh, ratio_map):
    energy = fresh.astype(jnp.float32).reshape(NDIR, NFREQ, -1)
    theta = angle_of(jnp.arange(NDIR, dtype=jnp.float32))
    cosine = jnp.cos(theta)
    sine = jnp.sin(theta)
    coeff = jnp.stack([cosine * cosine + 1.0, cosine * sine, sine * sine + 1.0])
    weighted = jnp.einsum("cd,dfn->cfn", coeff, energy, precision=lax.Precision.HIGHEST)
    total = jnp.sum(energy, axis=(0, 1))
    flat_ratio = ratio_map.reshape(NFREQ, -1)
    offset = jnp.array([0.5, 0.0, 0.5], dtype=jnp.float32)
    stress = (
        jnp.sum(flat_ratio[None] * weighted, axis=1) - offset[:, None] * total[None]
    ) * STRESS_SCALE
    return stress.reshape(3, fresh.shape[1], fresh.shape[2])


def forcing(stress_wide, currents, depth_map, maskf):
    slope_x = (stress_wide[:, 2:] - stress_wide[:, :-2]) * 0.5
    inner = stress_wide[:, 1:-1]
    padded_y = jnp.pad(inner, ((0, 0), (0, 0), (1, 1)))
    slope_y = (padded_y[:, :, 2:] - padded_y[:, :, :-2]) * 0.5
    force = jnp.stack([-(slope_x[0] + slope_y[1]), -(slope_x[1] + slope_y[2])])
    return maskf * (currents + force / depth_map)


def local(
    spectrum,
    land_mask,
    depth_class,
    upwind_signs,
    group_speed,
    speed_ratio,
    mixing,
    growth,
    wind_speed,
    water_depth,
    currents,
):
    bin_local = spectrum.shape[0]
    own_rows = currents.shape[1]
    device_index = lax.axis_index("bin")
    bin_ids = device_index * bin_local + jnp.arange(bin_local, dtype=jnp.int32)
    theta = angle_of((bin_ids // NFREQ).astype(jnp.float32))
    cos_abs = jnp.abs(jnp.cos(theta))[:, None, None]
    sin_abs = jnp.abs(jnp.sin(theta))[:, None, None]
    freq_select = (
        (bin_ids % NFREQ)[:, None] == jnp.arange(NFREQ, dtype=jnp.int32)[None, :]
    ).astype(jnp.float32)
    speed_table = jnp.dot(group_speed, freq_select.T, precision=lax.Precision.HIGHEST)
    classes = (depth_class[None] == jnp.arange(NCLASS, dtype=jnp.int32)[:, None, None]).astype(
        jnp.float32
    )
    celerity = jnp.einsum("kb,kxy->bxy", speed_table, classes, precision=lax.Precision.HIGHEST)
    upwind = lax.dynamic_slice_in_dim(upwind_signs, device_index * bin_local, bin_local, 1).astype(
        jnp.float32
    )
    maskf = land_mask.astype(jnp.float32)
    moved = upwind_step(
        spectrum.astype(jnp.float32),
        celerity,
        cos_abs,
        sin_abs,
        upwind[0][:, None, None],
        upwind[1][:, None, None],
        maskf,
    ).astype(jnp.bfloat16)
    first_row = device_index * own_rows
    wind_rows = lax.dynamic_slice_in_dim(wind_speed, first_row, own_rows, 0)
    class_rows = lax.dynamic_slice_in_dim(depth_class, first_row, own_rows, 0)
    mask_own = lax.dynamic_slice_in_dim(maskf, first_row, own_rows, 0)
    ratio_classes = (class_rows[None] == jnp.arange(NCLASS, dtype=jnp.int32)[:, None, None]).astype(
        jnp.float32
    )
    ratio_map = jnp.einsum(
        "kf,kxy->fxy", speed_ratio, ratio_classes, precision=lax.Precision.HIGHEST
    )

    def owner_step(received, wind_block):
        energy = received.astype(jnp.float32).reshape(received.shape[0], -1)
        return integrate(energy, mixing, growth, wind_block.reshape(-1)).reshape(received.shape)

    pieces = [(lax.all_to_all(moved, "bin", split_axis=1, concat_axis=0, tiled=True), wind_rows)]
    fresh = jnp.concatenate([owner_step(piece, wind_part) for piece, wind_part in pieces], axis=2)
    stress = extended(radiation(fresh, ratio_map), (("bin", 1),), 1)
    spectrum_next = lax.all_to_all(fresh, "bin", split_axis=0, concat_axis=1, tiled=True)
    depth_map = jnp.einsum("k,kxy->xy", water_depth, ratio_classes, precision=lax.Precision.HIGHEST)
    return (spectrum_next, forcing(stress, currents, depth_map, mask_own))


CHUNKS = 2
PLANES = 4
GROUP = 16
LANES = 128
COEF_ROWS = 160
MESH = pl.DeviceIdType.MESH
HIGHEST = lax.Precision.HIGHEST


def flipped(index, k, n):
    result, bit = 0, 1
    while bit < n:
        result = result + ((index // bit + k // bit) % 2) * bit
        bit *= 2
    return result


def stress_matrix():
    theta = angle_of(np.arange(NDIR, dtype=np.float64))
    cosine, sine = np.cos(theta), np.sin(theta)
    weights = np.stack([cosine * cosine + 1.0, cosine * sine, sine * sine + 1.0])
    full = np.repeat(weights, NFREQ, axis=1)
    high = full.astype(jnp.bfloat16).astype(np.float64)
    table = np.ones((8, NDIR * NFREQ), dtype=np.float32)
    table[:3] = high
    table[3:6] = (full - high).astype(jnp.bfloat16)
    return table


def trig_table():
    theta = angle_of(np.arange(NDIR, dtype=np.float64))
    return np.abs(np.stack([np.cos(theta), np.sin(theta)])).astype(np.float32)


def turning(outer, inner):
    side = outer * inner
    row_id = lax.broadcasted_iota(jnp.int32, (side, side), 0)
    col_id = lax.broadcasted_iota(jnp.int32, (side, side), 1)
    hit = (row_id // inner == col_id % outer) & (row_id % inner == col_id // outer)
    return jnp.where(hit, 1.0, 0.0).astype(jnp.bfloat16)


def wide(tile, width):
    return jnp.concatenate([tile] * (width // LANES), axis=1)


def fused_kernel(
    n,
    spectrum_hbm,
    mask_hbm,
    class_hbm,
    signs_hbm,
    speed_hbm,
    ratio_hbm,
    mixing_hbm,
    growth_hbm,
    wind_hbm,
    depth_hbm,
    currents_hbm,
    trig_hbm,
    weight_hbm,
    back,
    currents_out_hbm,
    currents_out,
    spectrum_v,
    mask_ref,
    class_ref,
    signs_ref,
    speed_ref,
    ratio_ref,
    mixing_v,
    growth_ref,
    wind_ref,
    depth_ref,
    currents_ref,
    trig_ref,
    weight_ref,
    coef_v,
    perm,
    energy_v,
    flux,
    speed_cols,
    sign_cols,
    growth_cols,
    ratio_map,
    send,
    state,
    total,
    stress,
    halo,
    load_sems,
    store_sems,
    fwd_send,
    fwd_recv,
    ret_send,
    ret_recv,
    halo_send,
    halo_recv,
    relay,
):
    me = lax.axis_index("bin")
    nb, nx, ny = spectrum_v.shape
    bins = mixing_v.shape[0]
    width = ny // CHUNKS
    groups = nb // GROUP

    loads = [
        pltpu.make_async_copy(src, dst, load_sems.at[i])
        for i, (src, dst) in enumerate(
            [
                (spectrum_hbm, spectrum_v),
                (speed_hbm, speed_ref),
                (signs_hbm, signs_ref),
                (trig_hbm, trig_ref),
                (mask_hbm, mask_ref),
                (class_hbm, class_ref),
                (growth_hbm, growth_ref.at[0]),
                (ratio_hbm, ratio_ref),
                (wind_hbm, wind_ref),
                (mixing_hbm, mixing_v),
                (weight_hbm, weight_ref),
                (depth_hbm, depth_ref),
                (currents_hbm, currents_ref),
            ]
        )
    ]
    for load in loads:
        load.start()
    barrier = pltpu.get_barrier_semaphore()

    span = n // PLANES
    plane = me // span
    inner = (plane > 0) & (plane < PLANES - 1)
    outer = (plane == 0) | (plane == PLANES - 1)
    outward = jnp.where(plane == 1, me - span, me + span)
    inward = jnp.where(plane == 1, me + span, me - span)

    def tell(semaphore, device):
        pl.semaphore_signal(semaphore, inc=1, device_id={"bin": device}, device_id_type=MESH)

    def greet_lower(q, carry):
        tell(barrier, (plane - 1) * span + q)
        return carry

    def greet_upper(q, carry):
        tell(barrier, (plane + 1) * span + q)
        return carry

    def greet_own(k, carry):
        tell(barrier, flipped(me, k, n))
        return carry

    @pl.when(plane > 0)
    def _():
        lax.fori_loop(0, span, greet_lower, 0)

    @pl.when(plane < PLANES - 1)
    def _():
        lax.fori_loop(0, span, greet_upper, 0)

    lax.fori_loop(1, span, greet_own, 0)

    for load in loads[1:4]:
        load.wait()
    side = GROUP * nx
    perm[...] = turning(nx, GROUP)
    spread = jnp.where(
        lax.broadcasted_iota(jnp.int32, (NCLASS, NCLASS * LANES), 0)
        == lax.broadcasted_iota(jnp.int32, (NCLASS, NCLASS * LANES), 1) // LANES,
        1.0,
        0.0,
    )
    columns = lax.dot_general(
        speed_ref[...], spread, (((0,), (0,)), ((), ())), precision=HIGHEST,
        preferred_element_type=jnp.float32,
    )
    columns = jnp.concatenate([columns] * (nb // NFREQ), axis=0)
    for k in range(NCLASS):
        speed_cols[k] = columns[:, k * LANES : (k + 1) * LANES]
    pick = jnp.where(
        lax.broadcasted_iota(jnp.int32, (nb, bins), 1)
        == lax.broadcasted_iota(jnp.int32, (nb, bins), 0) + me * nb,
        1.0,
        0.0,
    ).astype(jnp.bfloat16)
    for axis in range(2):
        signs = jnp.broadcast_to(
            signs_ref[axis : axis + 1, :].astype(jnp.float32), (LANES, bins)
        ).astype(jnp.bfloat16)
        sign_cols[axis] = lax.dot_general(
            pick, signs, (((1,), (1,)), ((), ())), preferred_element_type=jnp.float32
        )
    per_dev = nb // NFREQ
    bin_row = lax.broadcasted_iota(jnp.int32, (nb, LANES), 0)
    for axis in range(2):
        column = jnp.zeros((nb, LANES), jnp.float32)
        for d in range(per_dev):
            column = jnp.where(bin_row // NFREQ == d, trig_ref[axis, me * per_dev + d], column)
        sign_cols[2 + axis] = column

    flux[0] = jnp.zeros((nb, ny), jnp.float32)
    flux[nx + 1] = jnp.zeros((nb, ny), jnp.float32)

    loads[0].wait()
    for g in range(groups):
        block = spectrum_v[g * GROUP : (g + 1) * GROUP].reshape(side, ny)
        turned = jnp.dot(perm[...], block, preferred_element_type=jnp.float32)
        energy_v[:, g * GROUP : (g + 1) * GROUP, :] = turned.astype(jnp.bfloat16).reshape(
            nx, GROUP, ny
        )

    loads[4].wait()
    loads[5].wait()

    def flux_row(i, carry):
        sea = jnp.where(mask_ref[pl.ds(i, 1), :] > 0, class_ref[pl.ds(i, 1), :], -1)
        sea = jnp.broadcast_to(sea, (GROUP, ny))
        for g in range(groups):
            rows = slice(g * GROUP, (g + 1) * GROUP)
            celerity = jnp.zeros((GROUP, ny), jnp.float32)
            for k in range(NCLASS):
                celerity = jnp.where(sea == k, wide(speed_cols[k, rows, :], ny), celerity)
            flux[i + 1, rows, :] = celerity * energy_v[i, rows, :].astype(jnp.float32)
        return carry

    lax.fori_loop(0, nx, flux_row, 0)

    @pl.when(outer)
    def _():
        pl.semaphore_wait(barrier, 2 * span - 1)

    @pl.when(inner)
    def _():
        pl.semaphore_wait(barrier, 3 * span - 1)
        tell(relay.at[0], inward)
        tell(relay.at[0], outward)

    def far_first(t):
        stage = t // span
        block = PLANES - 1 - stage
        block = jnp.where(inner & (stage < 2), PLANES - 2 + stage, block)
        return block * span + span - 1 - t % span

    def forward(c, k):
        return pltpu.make_async_remote_copy(
            src_ref=send.at[c, flipped(me, k, n)],
            dst_ref=state.at[c, 0, pl.ds(pl.multiple_of(me * nb, nb), nb), :],
            send_sem=fwd_send.at[c, k],
            recv_sem=fwd_recv.at[c, k],
            device_id={"bin": flipped(me, k, n)},
            device_id_type=MESH,
        )

    def backward(c, k):
        return pltpu.make_async_remote_copy(
            src_ref=state.at[c, 0, pl.ds(pl.multiple_of(flipped(me, k, n) * nb, nb), nb), :],
            dst_ref=back.at[c, me],
            send_sem=ret_send.at[c, k],
            recv_sem=ret_recv.at[c, k],
            device_id={"bin": flipped(me, k, n)},
            device_id_type=MESH,
        )

    def keep(c):
        return pltpu.make_async_copy(
            state.at[c, 0, pl.ds(pl.multiple_of(me * nb, nb), nb), :],
            back.at[c, me],
            store_sems.at[c],
        )

    lane = lax.broadcasted_iota(jnp.int32, (GROUP, ny), 1)

    def moved_row(t, carry):
        stage = t // span
        block = jnp.where(
            inner,
            PLANES - 1 - stage,
            jnp.where(stage == PLANES - 1, 0, stage + 1),
        )
        k = block * span + span - 1 - t % span
        j = flipped(me, k, n)
        maskf = mask_ref[pl.ds(j, 1), :].astype(jnp.float32)
        for g in range(groups):
            rows = slice(g * GROUP, (g + 1) * GROUP)
            sign_x = wide(sign_cols[0, rows, :], ny)
            sign_y = wide(sign_cols[1, rows, :], ny)
            cos_abs = wide(sign_cols[2, rows, :], ny)
            sin_abs = wide(sign_cols[3, rows, :], ny)
            here = flux[j + 1, rows, :]
            lower_y = jnp.where(lane == 0, 0.0, pltpu.roll(here, 1, 1))
            upper_y = jnp.where(lane == ny - 1, 0.0, pltpu.roll(here, ny - 1, 1))
            beside_x = jnp.where(sign_x > 0, flux[j, rows, :], flux[j + 2, rows, :])
            beside_y = jnp.where(sign_y > 0, lower_y, upper_y)
            energy = energy_v[j, rows, :].astype(jnp.float32)
            moved = maskf * (
                energy - cos_abs * (here - beside_x) - sin_abs * (here - beside_y)
            )
            moved = moved.astype(jnp.bfloat16)
            for c in range(CHUNKS):
                send[c, j, rows, :] = moved[:, c * width : (c + 1) * width]

        @pl.when(t == span)
        def _():
            pl.semaphore_wait(relay.at[0], 1)

            @pl.when(inner)
            def _():
                tell(relay.at[1], outward)

        @pl.when((t == 2 * span) & outer)
        def _():
            pl.semaphore_wait(relay.at[1], 1)

        @pl.when(k > 0)
        def _():
            forward(0, k).start()

        return carry

    lax.fori_loop(0, n, moved_row, 0)
    for c in range(1, CHUNKS):

        def start_forward(t, carry):
            forward(c, n - 1 - t).start()
            return carry

        lax.fori_loop(0, n - 1, start_forward, 0)
    own = pl.ds(pl.multiple_of(me * nb, nb), nb)
    for c in range(CHUNKS):
        state[c, 0, own, :] = send[c, me]

    for load in loads[6:]:
        load.wait()
    growth_cols[...] = jnp.broadcast_to(growth_ref[...], (LANES, bins)).T
    class_row = class_ref[pl.ds(me, 1), :]
    one_hot = jnp.where(
        lax.broadcasted_iota(jnp.int32, (NCLASS, ny), 0)
        == jnp.broadcast_to(class_row, (NCLASS, ny)),
        1.0,
        0.0,
    )
    ratio_map[...] = lax.dot_general(
        ratio_ref[...], one_hot, (((0,), (0,)), ((), ())), precision=HIGHEST,
        preferred_element_type=jnp.float32,
    )
    stress[...] = jnp.zeros_like(stress)
    same_freq = (
        lax.broadcasted_iota(jnp.int32, (NFREQ, bins), 1) % NFREQ
        == lax.broadcasted_iota(jnp.int32, (NFREQ, bins), 0)
    )
    weights = [jnp.where(same_freq, weight_ref[i : i + 1, :], 0.0) for i in range(6)]
    ones = jnp.broadcast_to(weight_ref[6:7, :], (COEF_ROWS - 6 * NFREQ, bins))
    coef_v[...] = jnp.concatenate(weights + [ones], axis=0).astype(jnp.bfloat16)

    @pl.when(me == 0)
    def _():
        halo[0] = jnp.zeros_like(halo[0])

    @pl.when(me == n - 1)
    def _():
        halo[1] = jnp.zeros_like(halo[1])

    tall = 256
    for c in range(CHUNKS):
        lanes = slice(c * width, (c + 1) * width)

        def wait_forward(k, carry):
            forward(c, k).wait_recv()
            return carry

        lax.fori_loop(1, n, wait_forward, 0)
        wind = wind_ref[pl.ds(me, 1), lanes]
        total[...] = state[c, 0].astype(jnp.float32)

        def substep(s, carry):
            now = s % 2
            rounded = state[c, now]
            for r in range(0, bins, tall):
                mixed = jnp.dot(
                    mixing_v[r : r + tall, :], rounded, preferred_element_type=jnp.float32
                )
                held = total[r : r + tall, :]
                held = held + mixed + wide(growth_cols[r : r + tall, :], width) * wind * held
                total[r : r + tall, :] = held
                state[c, 1 - now, r : r + tall, :] = held.astype(jnp.bfloat16)
            return carry

        lax.fori_loop(0, SUBS, substep, 0)

        def start_backward(t, carry):
            backward(c, far_first(t)).start()
            return carry

        lax.fori_loop(0, n - 1, start_backward, 0)
        keep(c).start()
        weighted = jnp.dot(coef_v[...], state[c, 0], preferred_element_type=jnp.float32)
        whole_sum = weighted[6 * NFREQ : 6 * NFREQ + 1, :]
        for comp, offset in enumerate((0.5, 0.0, 0.5)):
            first = comp * NFREQ
            second = (3 + comp) * NFREQ
            part = weighted[first : first + NFREQ, :] + weighted[second : second + NFREQ, :]
            part = jnp.sum(ratio_map[:, lanes] * part, axis=0, keepdims=True)
            stress[comp : comp + 1, lanes] = (part - offset * whole_sum) * STRESS_SCALE

    def to_next():
        return pltpu.make_async_remote_copy(
            src_ref=stress,
            dst_ref=halo.at[0],
            send_sem=halo_send.at[0],
            recv_sem=halo_recv.at[0],
            device_id={"bin": (me + 1) % n},
            device_id_type=MESH,
        )

    def to_previous():
        return pltpu.make_async_remote_copy(
            src_ref=stress,
            dst_ref=halo.at[1],
            send_sem=halo_send.at[1],
            recv_sem=halo_recv.at[1],
            device_id={"bin": (me + n - 1) % n},
            device_id_type=MESH,
        )

    @pl.when(me < n - 1)
    def _():
        to_next().start()

    @pl.when(me > 0)
    def _():
        to_previous().start()

    @pl.when(me > 0)
    def _():
        to_next().wait_recv()

    @pl.when(me < n - 1)
    def _():
        to_previous().wait_recv()

    slope_x = (halo[1] - halo[0]) * 0.5
    mine = stress[...]
    lane8 = lax.broadcasted_iota(jnp.int32, mine.shape, 1)
    above = jnp.where(lane8 == ny - 1, 0.0, pltpu.roll(mine, ny - 1, 1))
    below = jnp.where(lane8 == 0, 0.0, pltpu.roll(mine, 1, 1))
    slope_y = (above - below) * 0.5
    depth = jnp.zeros((1, ny), jnp.float32)
    for k in range(NCLASS):
        depth = jnp.where(class_row == k, depth_ref[k], depth)
    sea_row = mask_ref[pl.ds(me, 1), :].astype(jnp.float32)
    for comp in range(2):
        force = -(slope_x[comp : comp + 1, :] + slope_y[comp + 1 : comp + 2, :])
        currents_out[comp] = sea_row * (currents_ref[comp] + force / depth)

    store_currents = pltpu.make_async_copy(
        currents_out, currents_out_hbm, store_sems.at[CHUNKS]
    )
    store_currents.start()

    def wait_backward(k, carry):
        for c in range(CHUNKS):
            backward(c, k).wait_recv()
        return carry

    lax.fori_loop(1, n, wait_backward, 0)

    def finish(k, carry):
        for c in range(CHUNKS):
            forward(c, k).wait_send()
            backward(c, k).wait_send()
        return carry

    lax.fori_loop(1, n, finish, 0)

    @pl.when(me < n - 1)
    def _():
        to_next().wait_send()

    @pl.when(me > 0)
    def _():
        to_previous().wait_send()

    store_currents.wait()
    for c in range(CHUNKS):
        keep(c).wait()


def fused(
    n,
    spectrum,
    land_mask,
    depth_class,
    upwind_signs,
    group_speed,
    speed_ratio,
    mixing,
    growth,
    wind_speed,
    water_depth,
    currents,
):
    nb, nx, ny = spectrum.shape
    bins = mixing.shape[0]
    width = ny // CHUNKS
    hbm = pl.BlockSpec(memory_space=pltpu.HBM)
    f32, bf16 = jnp.float32, jnp.bfloat16
    dma = pltpu.SemaphoreType.DMA
    return pl.pallas_call(
        functools.partial(fused_kernel, n),
        out_shape=(
            jax.ShapeDtypeStruct((CHUNKS, nx, nb, width), bf16),
            jax.ShapeDtypeStruct(currents.shape, f32),
        ),
        in_specs=[hbm] * 13,
        out_specs=(hbm, hbm),
        scratch_shapes=[
            pltpu.VMEM(currents.shape, f32),
            pltpu.VMEM((nb, nx, ny), bf16),
            pltpu.VMEM(land_mask.shape, jnp.int32),
            pltpu.VMEM(depth_class.shape, jnp.int32),
            pltpu.VMEM(upwind_signs.shape, jnp.int32),
            pltpu.VMEM(group_speed.shape, f32),
            pltpu.VMEM(speed_ratio.shape, f32),
            pltpu.VMEM((bins, bins), bf16),
            pltpu.VMEM((1, bins), f32),
            pltpu.VMEM(wind_speed.shape, f32),
            pltpu.SMEM(water_depth.shape, f32),
            pltpu.VMEM(currents.shape, f32),
            pltpu.SMEM((2, NDIR), f32),
            pltpu.VMEM((8, bins), f32),
            pltpu.VMEM((COEF_ROWS, bins), bf16),
            pltpu.VMEM((GROUP * nx, GROUP * nx), bf16),
            pltpu.VMEM((nx, nb, ny), bf16),
            pltpu.VMEM((nx + 2, nb, ny), f32),
            pltpu.VMEM((NCLASS, nb, LANES), f32),
            pltpu.VMEM((4, nb, LANES), f32),
            pltpu.VMEM((bins, LANES), f32),
            pltpu.VMEM((NFREQ, ny), f32),
            pltpu.VMEM((CHUNKS, nx, nb, width), bf16),
            pltpu.VMEM((CHUNKS, 2, bins, width), bf16),
            pltpu.VMEM((bins, width), f32),
            pltpu.VMEM((8, ny), f32),
            pltpu.VMEM((2, 8, ny), f32),
            dma((13,)),
            dma((CHUNKS + 1,)),
            dma((CHUNKS, n)),
            dma((CHUNKS, n)),
            dma((CHUNKS, n)),
            dma((CHUNKS, n)),
            dma((2,)),
            dma((2,)),
            pltpu.SemaphoreType.REGULAR((2,)),
        ],
        compiler_params=pltpu.CompilerParams(
            collective_id=0, has_side_effects=True, vmem_limit_bytes=64 * 1024 * 1024
        ),
    )(
        spectrum,
        land_mask,
        depth_class,
        upwind_signs,
        group_speed,
        speed_ratio,
        mixing,
        growth,
        wind_speed,
        water_depth,
        currents,
        jnp.asarray(trig_table()),
        jnp.asarray(stress_matrix()),
    )


def turn_kernel(back, currents_in, fresh_out, currents_out, back_v, fresh_v, currents_v, sems):
    chunks, nx, nb, width = back_v.shape
    groups = [pl.ds(g, GROUP) for g in range(0, nb, GROUP)]
    loads = [pltpu.make_async_copy(back.at[c], back_v.at[c], sems.at[0, c]) for c in range(chunks)]
    stores = [
        pltpu.make_async_copy(fresh_v.at[g], fresh_out.at[g], sems.at[1, i])
        for i, g in enumerate(groups)
    ]
    load_currents = pltpu.make_async_copy(currents_in, currents_v, sems.at[0, chunks])
    store_currents = pltpu.make_async_copy(currents_v, currents_out, sems.at[1, len(groups)])
    for load in loads:
        load.start()
    load_currents.start()
    perm = turning(GROUP, nx)
    load_currents.wait()
    store_currents.start()
    for load in loads:
        load.wait()
    for g, store in zip(groups, stores):
        for c in range(chunks):
            block = back_v[c, :, g, :].reshape(nx * GROUP, width)
            turned = jnp.dot(perm, block, preferred_element_type=jnp.float32)
            fresh_v[g, :, c * width : (c + 1) * width] = turned.astype(jnp.bfloat16).reshape(
                GROUP, nx, width
            )
        store.start()
    for store in stores + [store_currents]:
        store.wait()


def turn(back, currents):
    chunks, nx, nb, width = back.shape
    hbm = pl.BlockSpec(memory_space=pltpu.HBM)
    fresh = jax.ShapeDtypeStruct((nb, nx, chunks * width), back.dtype)
    count = max(chunks, nb // GROUP) + 1
    return pl.pallas_call(
        turn_kernel,
        out_shape=(fresh, jax.ShapeDtypeStruct(currents.shape, currents.dtype)),
        in_specs=[hbm, hbm],
        out_specs=(hbm, hbm),
        scratch_shapes=[
            pltpu.VMEM(back.shape, back.dtype),
            pltpu.VMEM(fresh.shape, fresh.dtype),
            pltpu.VMEM(currents.shape, currents.dtype),
            pltpu.SemaphoreType.DMA((2, count)),
        ],
        compiler_params=pltpu.CompilerParams(vmem_limit_bytes=64 * 1024 * 1024),
    )(back, currents)


def fits(n, nb, nx, ny, rows):
    return (
        n & (n - 1) == 0
        and n >= 2 * PLANES
        and rows == 1
        and nx % GROUP == 0
        and nb % GROUP == 0
        and nb % NFREQ == 0
        and ny % (CHUNKS * LANES) == 0
    )


def on_device(*arrays):
    n = lax.axis_size("bin")
    nb, nx, ny = arrays[0].shape
    if fits(n, nb, nx, ny, arrays[-1].shape[1]):
        return turn(*fused(n, *arrays))
    return local(*arrays)


def solution(mesh):
    in_specs = (
        P(("ens", "bin"), None, None),
        P(),
        P(),
        P(),
        P(),
        P(),
        P(),
        P(),
        P("ens", None),
        P(),
        P("ens", "bin", None),
    )
    out_specs = (P(("ens", "bin"), None, None), P("ens", "bin", None))
    return jax.shard_map(on_device, mesh=mesh, in_specs=in_specs, out_specs=out_specs, check_vma=False)
```
